32 devices in a mesh: cells: 32 (over z, y, x, core).
Axes of the slice: x: 2, y: 2, z: 4, core: 2. Of those that a mesh axis runs over, the one named last changes fastest.
Arguments:
- multipoles: bfloat16 [216, 32768], P(None, 'cells'), may hold values from -6 to 6
- compress: bfloat16 [216, 128], replicated, may hold values from -0.4375 to 0.4375
- operators: bfloat16 [316, 128, 128], replicated, may hold values from -0.0390625 to 0.0390625
- expand: bfloat16 [128, 216], replicated, may hold values from -0.5 to 0.5
Outputs:
- local_field: float32 [216, 32768], P(None, 'cells')
The draws below stay inside these ranges and needn't reach their ends.
All inputs are finite; a program needn't handle non-finite values.
Results may differ from the reference program's by a relative error of at most 0.0041.
Values may be sent and summed in bfloat16 or wider, within the bound.
A program may use at most 256 MiB of HBM per device.

```python
import jax
import jax.numpy as jnp
import numpy as np
from jax import lax

CHEB = 216
RANK = 128
OFFSETS = 316
LIST = 189
CELLS = 32768


def block_levels(own_key, extent, cuts, smallest, largest):
    def one(axis_at, blocks):
        heights = jax.random.uniform(jax.random.fold_in(jax.random.fold_in(own_key, 6), axis_at), (blocks,), jnp.float32, smallest / len(cuts), largest / len(cuts))
        return jnp.repeat(jnp.exp(heights), extent[axis_at] // blocks).reshape((-1,) + (1,) * (len(extent) - axis_at - 1))

    factor_of = one(*cuts[0])
    for cut in cuts[1:]:
        factor_of = factor_of * one(*cut)
    return factor_of


def bell_draw(key, shape, scale, limit, cuts=(), kind=jnp.bfloat16):
    values = scale * jax.random.normal(key, shape, jnp.float32)
    if cuts:
        values = values * block_levels(key, shape, cuts, -0.22, 0.18)
    return jnp.clip(values, -limit, limit).astype(kind)


def setup_inputs(seed: int = 0) -> dict:
    splits = jax.random.split(jax.random.key(seed), 5)
    return {
        "multipoles": bell_draw(splits[0], (CHEB, CELLS), 1.0, 6.0, ((1, 32),)),
        "compress": bell_draw(splits[1], (CHEB, RANK), CHEB ** -0.5, 0.4375),
        "operators": bell_draw(splits[2], (OFFSETS, RANK, RANK), (LIST * RANK) ** -0.5, 0.0390625),
        "expand": bell_draw(splits[3], (RANK, CHEB), RANK ** -0.5, 0.5),
    }


def offset_list():
    result = []
    for shift_x in range(-3, 4):
        for shift_y in range(-3, 4):
            for shift_z in range(-3, 4):
                if max(abs(shift_x), abs(shift_y), abs(shift_z)) >= 2:
                    result.append((shift_x, shift_y, shift_z))
    return result


def allowed_shifts(parity):
    return [shift for shift in range(-3, 4) if abs((parity + shift) // 2 - parity // 2) <= 1]


def grid_order(bit_count):
    axes_by_dim = [[axis_number for axis_number in range(bit_count) if (bit_count - 1 - axis_number) % 3 == dimension] for dimension in range(3)]
    order = axes_by_dim[0] + axes_by_dim[1] + axes_by_dim[2]
    return order, [len(entries) for entries in axes_by_dim]


def to_grid(flat_rows, bit_count):
    order, bit_totals = grid_order(bit_count)
    rank_width = flat_rows.shape[-1]
    shaped = flat_rows.reshape([2] * bit_count + [rank_width])
    shaped = jnp.transpose(shaped, order + [bit_count])
    return shaped.reshape([2 ** bit_total for bit_total in bit_totals] + [rank_width])


def to_flat(grid_rows, bit_count):
    order, bit_totals = grid_order(bit_count)
    rank_width = grid_rows.shape[-1]
    shaped = grid_rows.reshape([2] * bit_count + [rank_width])
    inverse = [int(entry) for entry in np.argsort(np.array(order))] + [bit_count]
    return jnp.transpose(shaped, inverse).reshape(2 ** bit_count, rank_width)


def reference(multipoles, compress, operators, expand):
    bit_count = CELLS.bit_length() - 1
    compressed = lax.dot_general(multipoles, compress, (((0,), (0,)), ((), ())), preferred_element_type=jnp.float32).astype(jnp.bfloat16)
    grid_field = to_grid(compressed.astype(jnp.float32), bit_count)
    side_x, side_y, side_z, rank_width = grid_field.shape
    half_x, half_y, half_z = side_x // 2, side_y // 2, side_z // 2
    padded = jnp.pad(grid_field, ((2, 2), (2, 2), (2, 2), (0, 0)))
    parity_split = padded.reshape(half_x + 2, 2, half_y + 2, 2, half_z + 2, 2, rank_width)
    weights = operators.astype(jnp.float32)
    lookup = {triple: offset_id for offset_id, triple in enumerate(offset_list())}
    pieces = []
    for parity_x in range(2):
        for parity_y in range(2):
            for parity_z in range(2):
                starts = []
                offset_ids = []
                for shift_x in allowed_shifts(parity_x):
                    for shift_y in allowed_shifts(parity_y):
                        for shift_z in allowed_shifts(parity_z):
                            triple = (shift_x, shift_y, shift_z)
                            if triple in lookup:
                                start_x = 2 + parity_x + shift_x
                                start_y = 2 + parity_y + shift_y
                                start_z = 2 + parity_z + shift_z
                                starts.append([start_x // 2, start_x % 2, start_y // 2, start_y % 2, start_z // 2, start_z % 2])
                                offset_ids.append(lookup[triple])
                start_table = jnp.asarray(np.array(starts, dtype=np.int32))
                id_table = jnp.asarray(np.array(offset_ids, dtype=np.int32))

                def accumulate(summed, entry_pair):
                    start_row, offset_id = entry_pair
                    source = lax.dynamic_slice(parity_split, (start_row[0], start_row[1], start_row[2], start_row[3], start_row[4], start_row[5], jnp.int32(0)), (half_x, 1, half_y, 1, half_z, 1, rank_width))
                    source = source.reshape(half_x * half_y * half_z, rank_width)
                    matrix = lax.dynamic_index_in_dim(weights, offset_id, 0, keepdims=False)
                    return summed + jnp.dot(source, matrix, precision=lax.Precision.HIGHEST, preferred_element_type=jnp.float32), None

                initial = jnp.zeros((half_x * half_y * half_z, rank_width), jnp.float32)
                summed, unused = lax.scan(accumulate, initial, (start_table, id_table))
                pieces.append(summed.reshape(half_x, half_y, half_z, rank_width))
    stacked = jnp.stack(pieces).reshape(2, 2, 2, half_x, half_y, half_z, rank_width)
    whole_grid = jnp.transpose(stacked, (3, 0, 4, 1, 5, 2, 6)).reshape(side_x, side_y, side_z, rank_width)
    reduced = to_flat(whole_grid, bit_count).astype(jnp.bfloat16)
    return lax.dot_general(expand, reduced, (((0,), (1,)), ((), ())), preferred_element_type=jnp.float32)
```

```python
import functools

import jax
import jax.numpy as jnp
import numpy as np
from jax import lax
from jax.experimental import pallas as pl
from jax.experimental.pallas import tpu as pltpu
from jax.sharding import PartitionSpec as P

SIDE = (8, 4, 4)
PLANE = SIDE[1] * SIDE[2]
FLAT = [(0, 1, 0), (0, -1, 0), (0, 0, 1), (0, 0, -1), (0, 1, 1), (0, 1, -1), (0, -1, 1), (0, -1, -1)]
SLANT = [(ex, ey, ez) for ex in (-1, 1) for ey in (-1, 0, 1) for ez in (-1, 0, 1)]
WAYS = FLAT + SLANT


def slot_table():
    table, start = {}, 0
    for way in WAYS:
        rows = 32 if way in FLAT[:4] else 16
        table[way] = (start, rows)
        start += rows
    return table, start


SLOTS, SLOT_ROWS = slot_table()
FLAT_ROWS = SLOTS[SLANT[0]][0]


def offset_table():
    table = {}
    for sx in range(-3, 4):
        for sy in range(-3, 4):
            for sz in range(-3, 4):
                if max(abs(sx), abs(sy), abs(sz)) >= 2:
                    table[(sx, sy, sz)] = len(table)
    return table


def parent_place(morton):
    coords = [0, 0, 0]
    for bit in range(7):
        coords[bit % 3] += (morton >> bit & 1) << (bit // 3)
    return (coords[0] * SIDE[1] + coords[1]) * SIDE[2] + coords[2]


def picks():
    table = np.zeros((SIDE[0] + 2, 9 * PLANE, 256), np.float32)
    for plane in range(SIDE[0] + 2):
        x = plane - 1
        row = 0
        for dz in (-1, 0, 1):
            for dy in (-1, 0, 1):
                for y in range(SIDE[1]):
                    for z in range(SIDE[2]):
                        sy, sz = y + dy, z + dz
                        ey = -1 if sy < 0 else 1 if sy >= SIDE[1] else 0
                        ez = -1 if sz < 0 else 1 if sz >= SIDE[2] else 0
                        wy, wz = sy % SIDE[1], sz % SIDE[2]
                        if x < 0 or x >= SIDE[0]:
                            block = (ey + 1) * 3 + ez + 1
                            column = block * PLANE + wy * SIDE[2] + wz
                        elif ey == 0 and ez == 0:
                            column = FLAT_ROWS + wy * SIDE[2] + wz
                        else:
                            start = SLOTS[(0, ey, ez)][0]
                            line = wz if ez == 0 else wy if ey == 0 else 0
                            column = start + line * SIDE[0] + x
                        table[plane, row, column] = 1
                        row += 1
    return table


def bits_of_dimension(device_count, local_bits):
    count = device_count.bit_length() - 1
    return [[bit for bit in range(count) if (local_bits + bit) % 3 == dim] for dim in range(3)]


def exchange_kernel(bit_lists, multipoles, compress, own, recv, field, send, send_sem, recv_sem):
    me = lax.axis_index("cells")
    position = []
    for bits in bit_lists:
        value = me * 0
        for rank, bit in enumerate(bits):
            value = value + (me // 2**bit) % 2 * 2**rank
        position.append(value)

    def neighbour(way):
        inside, device = None, me * 0
        for dim, bits in enumerate(bit_lists):
            place = position[dim] + way[dim]
            if way[dim]:
                fits = (place >= 0) & (place < 2 ** len(bits))
                inside = fits if inside is None else inside & fits
            for rank, bit in enumerate(bits):
                device = device + (place + 2 ** len(bits)) // 2**rank % 2 * 2**bit
        return inside, device

    ways = [way for way in WAYS if all(bits or not step for bits, step in zip(bit_lists, way))]
    near = {way: neighbour(way) for way in ways}
    barrier = pltpu.get_barrier_semaphore()
    for way in ways:
        inside, device = near[way]

        @pl.when(inside)
        def _():
            pl.semaphore_signal(barrier, inc=1, device_id=(device,), device_id_type=pl.DeviceIdType.MESH)

    compressed = lax.dot_general(
        multipoles[...], compress[...], (((0,), (0,)), ((), ())), preferred_element_type=jnp.float32
    )
    compressed = compressed.astype(jnp.bfloat16).astype(jnp.float32)
    for morton in range(SIDE[0] * PLANE):
        place = parent_place(morton)
        field[place * 8 : place * 8 + 8, :] = compressed[morton * 8 : morton * 8 + 8, :]

    def lanes(child):
        cx, cy, cz = child & 1, child >> 1 & 1, child >> 2
        start = (cx * 4 + cy * 2 + cz) * 128
        return slice(start, start + 128)

    for child in range(8):
        for x in range(SIDE[0]):
            rows = field[pl.ds(x * PLANE * 8 + child, PLANE, stride=8), :]
            own[x * PLANE : (x + 1) * PLANE, lanes(child)] = rows.astype(jnp.bfloat16)

    def column(y, z, child):
        return field[pl.ds((y * SIDE[2] + z) * 8 + child, SIDE[0], stride=PLANE * 8), :]

    for way in FLAT:
        start, rows = SLOTS[way]
        y = SIDE[1] - 1 if way[1] > 0 else 0
        z = SIDE[2] - 1 if way[2] > 0 else 0
        for child in range(8):
            if way[2] == 0:
                parts = [column(y, line, child) for line in range(SIDE[2])]
            elif way[1] == 0:
                parts = [column(line, z, child) for line in range(SIDE[1])]
            else:
                parts = [column(y, z, child)]
                parts.append(jnp.zeros_like(parts[0]))
            packed = jnp.concatenate(parts, axis=0).astype(jnp.bfloat16)
            send[start : start + rows, lanes(child)] = packed

    peers = me * 0
    for way in ways:
        peers = peers + jnp.where(near[way][0], 1, 0)
    pl.semaphore_wait(barrier, peers)

    def copy_to(way):
        start, rows = SLOTS[way]
        back = tuple(-step for step in way)
        target = SLOTS[back][0]
        if way[0]:
            x = SIDE[0] - 1 if way[0] > 0 else 0
            source = own.at[pl.ds(x * PLANE, PLANE)]
        else:
            source = send.at[pl.ds(start, rows)]
        return pltpu.make_async_remote_copy(
            src_ref=source,
            dst_ref=recv.at[pl.ds(target, rows)],
            send_sem=send_sem.at[WAYS.index(way)],
            recv_sem=recv_sem.at[WAYS.index(back)],
            device_id=(near[way][1],),
            device_id_type=pl.DeviceIdType.MESH,
        )

    for way in ways:

        @pl.when(near[way][0])
        def _():
            copy_to(way).start()

    for way in WAYS:
        start, rows = SLOTS[way]
        blank = jnp.zeros((rows, recv.shape[1]), recv.dtype)
        if way in near:

            @pl.when(jnp.logical_not(near[way][0]))
            def _():
                recv[start : start + rows, :] = blank
        else:
            recv[start : start + rows, :] = blank

    for way in ways:
        back = tuple(-step for step in way)

        @pl.when(near[way][0])
        def _():
            copy_to(way).wait_send()
            copy_to(back).wait_recv()


def interact_kernel(own, recv, pick, expand, operators, out, held, spread, total, flat, load_sem):
    offsets = offset_table()
    spans = {}
    for (sx, _, _), number in offsets.items():
        low, high = spans.get(sx, (number, number))
        spans[sx] = (min(low, number), max(high, number))

    def load(sx):
        low, high = spans[sx]
        rows = pl.ds(low, high - low + 1)
        return pltpu.make_async_copy(operators.at[rows], held.at[rows], load_sem.at[sx + 3])

    for sx in range(-3, 4):
        load(sx).start()

    for plane in range(SIDE[0] + 2):
        if 1 <= plane <= SIDE[0]:
            parts = [(recv, 0, FLAT_ROWS), (own, (plane - 1) * PLANE, PLANE)]
        else:
            parts = [(recv, SLOTS[SLANT[0 if plane == 0 else 9]][0], 9 * PLANE)]
        used = sum(part[2] for part in parts)
        for pair in range(4):
            lanes = slice(pair * 256, pair * 256 + 256)
            values = [ref[start : start + rows, lanes] for ref, start, rows in parts]
            values.append(jnp.zeros((256 - used, 256), jnp.bfloat16))
            copies = jnp.dot(
                pick[plane], jnp.concatenate(values, axis=0), preferred_element_type=jnp.float32
            ).astype(jnp.bfloat16)
            for dz in range(3):
                for dy in range(3):
                    row = (dz * 3 + dy) * PLANE
                    spread[pair, dy, plane, :, dz * 256 : dz * 256 + 256] = copies[row : row + PLANE, :]

    total[...] = jnp.zeros_like(total)
    for sx in range(-3, 4):
        load(sx).wait()
        for sy in range(-3, 4):
            weights, shifts = [], []
            for dz in (-1, 0, 1):
                lines = []
                for cz in (0, 1):
                    entries = []
                    for pz in (0, 1):
                        number = offsets.get((sx, sy, 2 * dz + cz - pz))
                        entries.append(None if number is None else held[number])
                    lines.append(entries)
                if all(entry is None for line in lines for entry in line):
                    continue
                blank = jnp.zeros((128, 128), jnp.bfloat16)
                for line in lines:
                    line = [blank if entry is None else entry for entry in line]
                    weights.append(jnp.concatenate(line, axis=1))
                shifts.append(dz + 1)
            weights = jnp.concatenate(weights, axis=0)
            classes, sources = [], []
            for px in (0, 1):
                for py in (0, 1):
                    dx, cx = (px + sx) // 2, (px + sx) % 2
                    dy, cy = (py + sy) // 2, (py + sy) % 2
                    if abs(dx) > 1 or abs(dy) > 1:
                        continue
                    source = spread[cx * 2 + cy, dy + 1, 1 + dx : 1 + dx + SIDE[0]]
                    source = source.reshape(SIDE[0] * PLANE, 768)
                    if len(shifts) < 3:
                        source = jnp.concatenate(
                            [source[:, dz * 256 : dz * 256 + 256] for dz in shifts], axis=1
                        )
                    classes.append(px * 2 + py)
                    sources.append(source)
            product = jnp.dot(
                jnp.concatenate(sources, axis=0), weights, preferred_element_type=jnp.float32
            )
            count = SIDE[0] * PLANE
            for number, kind in enumerate(classes):
                total[kind] += product[number * count : (number + 1) * count, :]

    for px in (0, 1):
        for py in (0, 1):
            for pz in (0, 1):
                child = px + 2 * py + 4 * pz
                rows = total[px * 2 + py, :, pz * 128 : pz * 128 + 128]
                flat[pl.ds(child, SIDE[0] * PLANE, stride=8), :] = rows
    places = [parent_place(morton) for morton in range(SIDE[0] * PLANE)]
    reduced = jnp.concatenate([flat[place * 8 : place * 8 + 8, :] for place in places], axis=0)
    out[...] = lax.dot_general(
        expand[...].T, reduced.astype(jnp.bfloat16), (((1,), (1,)), ((), ())),
        preferred_element_type=jnp.float32,
    )


def local(multipoles, compress, operators, expand):
    cells, rank = multipoles.shape[1], compress.shape[1]
    devices = lax.axis_size("cells")
    local_bits = cells.bit_length() - 1
    bit_lists = bits_of_dimension(devices, local_bits)
    vmem = pl.BlockSpec(memory_space=pltpu.VMEM)
    parents = SIDE[0] * PLANE
    own, recv = pl.pallas_call(
        functools.partial(exchange_kernel, bit_lists),
        out_shape=[
            jax.ShapeDtypeStruct((parents, 8 * rank), jnp.bfloat16),
            jax.ShapeDtypeStruct((SLOT_ROWS, 8 * rank), jnp.bfloat16),
        ],
        in_specs=[vmem] * 2,
        out_specs=[vmem] * 2,
        scratch_shapes=[
            pltpu.VMEM((cells, rank), jnp.float32),
            pltpu.VMEM((FLAT_ROWS, 8 * rank), jnp.bfloat16),
            pltpu.SemaphoreType.DMA((len(WAYS),)),
            pltpu.SemaphoreType.DMA((len(WAYS),)),
        ],
        compiler_params=pltpu.CompilerParams(
            collective_id=0, has_side_effects=True, vmem_limit_bytes=24 * 2**20
        ),
        name="halo_exchange",
    )(multipoles, compress)
    return pl.pallas_call(
        interact_kernel,
        out_shape=jax.ShapeDtypeStruct((expand.shape[1], cells), jnp.float32),
        in_specs=[vmem] * 4 + [pl.BlockSpec(memory_space=pl.ANY)],
        out_specs=vmem,
        scratch_shapes=[
            pltpu.VMEM(operators.shape, jnp.bfloat16),
            pltpu.VMEM((4, 3, SIDE[0] + 2, PLANE, 6 * rank), jnp.bfloat16),
            pltpu.VMEM((4, parents, 2 * rank), jnp.float32),
            pltpu.VMEM((cells, rank), jnp.float32),
            pltpu.SemaphoreType.DMA((7,)),
        ],
        compiler_params=pltpu.CompilerParams(vmem_limit_bytes=48 * 2**20),
        name="interactions",
    )(own, recv, jnp.asarray(picks(), jnp.bfloat16), expand, operators)


def solution(mesh):
    placed = (P(None, "cells"), P(), P(), P())
    return jax.shard_map(
        local, mesh=mesh, in_specs=placed, out_specs=P(None, "cells"), check_vma=False
    )
```

```python
import functools

import jax
import jax.numpy as jnp
import numpy as np
from jax import lax
from jax.experimental import pallas as pl
from jax.experimental.pallas import tpu as pltpu
from jax.sharding import PartitionSpec as P

SIDE_X, SIDE_Y, SIDE_Z = SIDE = (8, 4, 4)
PLANE = SIDE_X * SIDE_Y
PARENTS = PLANE * SIDE_Z
WAYS = [
    (ex, ey, ez)
    for ez in (0, -1, 1)
    for ey in (-1, 0, 1)
    for ex in (-1, 0, 1)
    if (ex, ey, ez) != (0, 0, 0)
]
PLACES = {
    (-1, 0, 0): ("face", 0, 16),
    (1, 0, 0): ("face", 16, 16),
    (0, -1, 0): ("face", 32, 32),
    (0, 1, 0): ("face", 64, 32),
    (0, 0, -1): ("face", 96, 32),
    (0, 0, 1): ("face", 128, 32),
}
for way in WAYS:
    if way not in PLACES:
        kind = "edge" if way[0] == 0 else "thin"
        PLACES[way] = (kind, sum(place[0] == kind for place in PLACES.values()), 16)
PAIR_WAYS = [(ex, ey) for ey in (-1, 1) for ex in (-1, 1)]


def offset_table():
    table = {}
    for sx in range(-3, 4):
        for sy in range(-3, 4):
            for sz in range(-3, 4):
                if max(abs(sx), abs(sy), abs(sz)) >= 2:
                    table[(sx, sy, sz)] = len(table)
    return table


def parent_place(morton):
    coords = [0, 0, 0]
    for bit in range(7):
        coords[bit % 3] += (morton >> bit & 1) << (bit // 3)
    return (coords[2] * SIDE_Y + coords[1]) * SIDE_X + coords[0]


def picks():
    table = np.zeros((SIDE_Z + 2, 9 * PLANE, 256), np.float32)
    for plane in range(SIDE_Z + 2):
        z = plane - 1
        outer = z < 0 or z >= SIDE_Z
        row = 0
        for dy in (-1, 0, 1):
            for dx in (-1, 0, 1):
                for y in range(SIDE_Y):
                    for x in range(SIDE_X):
                        sy, sx = y + dy, x + dx
                        ey = -1 if sy < 0 else 1 if sy >= SIDE_Y else 0
                        ex = -1 if sx < 0 else 1 if sx >= SIDE_X else 0
                        wy, wx = sy % SIDE_Y, sx % SIDE_X
                        if ex == 0 and ey == 0:
                            column = wy * SIDE_X + wx
                        elif ex == 0:
                            column = 32 + (ey > 0) * 8 + wx if outer else 32 + (ey > 0) * 32 + z * 8 + wx
                        elif ey == 0:
                            column = 48 + (ex > 0) * 4 + wy if outer else 96 + (ex > 0) * 16 + z * 4 + wy
                        else:
                            corner = PAIR_WAYS.index((ex, ey))
                            column = 56 + corner if outer else 128 + corner * 4 + z
                        table[plane, row, column] = 1
                        row += 1
    return table


def bits_of_dimension(device_count, local_bits):
    count = device_count.bit_length() - 1
    return [[bit for bit in range(count) if (local_bits + bit) % 3 == dim] for dim in range(3)]


def reduce_kernel(
    bit_lists, multipoles_hbm, compress_hbm, pick_hbm, operators, out,
    multipoles, compress, pick, held, field, own, face_out, edge_out, thin_out,
    face_in, edge_in, thin_in, rim, spread, total, load_sem, send_sem, recv_sem,
):
    offsets = offset_table()
    spans = {}
    for (sx, _, _), number in offsets.items():
        low, high = spans.get(sx, (number, number))
        spans[sx] = (min(low, number), max(high, number))

    def load_operators(sx):
        low, high = spans[sx]
        rows = pl.ds(low, high - low + 1)
        return pltpu.make_async_copy(operators.at[rows], held.at[rows], load_sem.at[sx + 6])

    load_multipoles = pltpu.make_async_copy(multipoles_hbm, multipoles, load_sem.at[0])
    load_compress = pltpu.make_async_copy(compress_hbm, compress, load_sem.at[1])
    load_pick = pltpu.make_async_copy(pick_hbm, pick, load_sem.at[2])
    load_multipoles.start()
    load_compress.start()
    load_pick.start()
    for sx in range(-3, 4):
        load_operators(sx).start()

    me = lax.axis_index("cells")
    position = []
    for bits in bit_lists:
        value = me * 0
        for rank, bit in enumerate(bits):
            value = value + (me // 2**bit) % 2 * 2**rank
        position.append(value)

    def neighbour(way):
        inside, device = None, me * 0
        for dim, bits in enumerate(bit_lists):
            place = position[dim] + way[dim]
            if way[dim]:
                fits = (place >= 0) & (place < 2 ** len(bits))
                inside = fits if inside is None else inside & fits
            for rank, bit in enumerate(bits):
                device = device + (place + 2 ** len(bits)) // 2**rank % 2 * 2**bit
        return inside, device

    ways = [way for way in WAYS if all(bits or not step for bits, step in zip(bit_lists, way))]
    near = {way: neighbour(way) for way in ways}
    barrier = pltpu.get_barrier_semaphore()
    peers = me * 0
    for way in ways:
        inside, device = near[way]
        peers = peers + jnp.where(inside, 1, 0)

        @pl.when(inside)
        def _():
            pl.semaphore_signal(barrier, inc=1, device_id=(device,), device_id_type=pl.DeviceIdType.MESH)

    def slot(buffers, way):
        kind, start, rows = PLACES[way]
        if kind == "face":
            return buffers[0].at[pl.ds(start, rows)]
        return buffers[1 if kind == "edge" else 2].at[start]

    inboxes = (face_in, edge_in, thin_in)
    for way in WAYS:
        target = slot(inboxes, way)
        if way in near:

            @pl.when(jnp.logical_not(near[way][0]))
            def _():
                target[...] = jnp.zeros(target.shape, target.dtype)
        else:
            target[...] = jnp.zeros(target.shape, target.dtype)
    rim[...] = jnp.zeros_like(rim)

    load_multipoles.wait()
    load_compress.wait()
    compressed = lax.dot_general(
        multipoles[...], compress[...], (((0,), (0,)), ((), ())), preferred_element_type=jnp.float32
    )
    compressed = compressed.astype(jnp.bfloat16).astype(jnp.float32)
    for morton in range(PARENTS):
        place = parent_place(morton)
        field[place * 8 : place * 8 + 8, :] = compressed[morton * 8 : morton * 8 + 8, :]

    def child_of(cx, cy, cz):
        return cx + 2 * cy + 4 * cz

    def line(place, child, count, step):
        return field[pl.ds(place * 8 + child, count, stride=step * 8), :]

    def pack(parts):
        return jnp.concatenate(parts, axis=0).astype(jnp.bfloat16)

    children = [(cx, cy, cz) for cx in (0, 1) for cy in (0, 1) for cz in (0, 1)]
    for number, bits in enumerate(children):
        child, lanes = child_of(*bits), slice(number * 128, number * 128 + 128)
        for z in range(SIDE_Z):
            own[z * PLANE : (z + 1) * PLANE, lanes] = line(z * PLANE, child, PLANE, 1).astype(jnp.bfloat16)
        for ex in (-1, 1):
            start = PLACES[(ex, 0, 0)][1]
            x = SIDE_X - 1 if ex > 0 else 0
            face_out[start : start + 16, lanes] = line(x, child, 16, SIDE_X).astype(jnp.bfloat16)
        for ey in (-1, 1):
            start = PLACES[(0, ey, 0)][1]
            y = SIDE_Y - 1 if ey > 0 else 0
            parts = [line(z * PLANE + y * SIDE_X, child, SIDE_X, 1) for z in range(SIDE_Z)]
            face_out[start : start + 32, lanes] = pack(parts)
    for way in WAYS:
        kind, start, _ = PLACES[way]
        x = SIDE_X - 1 if way[0] > 0 else 0
        y = SIDE_Y - 1 if way[1] > 0 else 0
        z = SIDE_Z - 1 if way[2] > 0 else 0
        place = z * PLANE + y * SIDE_X + x
        if kind == "edge":
            for cy in (0, 1):
                for cz in (0, 1):
                    parts = [line(place, child_of(cx, cy, cz), SIDE_X, 1) for cx in (0, 1)]
                    edge_out[start, :, (cy * 2 + cz) * 128 : (cy * 2 + cz + 1) * 128] = pack(parts)
        elif kind == "thin":
            for cz in (0, 1):
                parts = []
                for pair in range(4):
                    child = child_of(pair // 2, pair % 2, cz)
                    if way[2] == 0:
                        parts.append(line(place, child, SIDE_Z, PLANE))
                    elif way[1] == 0:
                        parts.append(line(place, child, SIDE_Y, SIDE_X))
                    else:
                        parts.append(field[place * 8 + child : place * 8 + child + 1, :])
                if way[1] and way[2]:
                    parts.append(jnp.zeros((12, 128), jnp.float32))
                thin_out[start, :, cz * 128 : cz * 128 + 128] = pack(parts)

    pl.semaphore_wait(barrier, peers)

    def copy_to(way):
        back = tuple(-step for step in way)
        if way[:2] == (0, 0):
            source = own.at[pl.ds(PARENTS - PLANE if way[2] > 0 else 0, PLANE)]
        else:
            source = slot((face_out, edge_out, thin_out), way)
        return pltpu.make_async_remote_copy(
            src_ref=source,
            dst_ref=slot(inboxes, back),
            send_sem=send_sem.at[WAYS.index(way)],
            recv_sem=recv_sem.at[WAYS.index(back)],
            device_id=(near[way][1],),
            device_id_type=pl.DeviceIdType.MESH,
        )

    for way in ways:

        @pl.when(near[way][0])
        def _():
            copy_to(way).start()

    def arrive(way):
        @pl.when(near[way][0])
        def _():
            copy_to(tuple(-step for step in way)).wait_recv()

    def spread_plane(plane, pair, values):
        used = sum(value.shape[0] for value in values)
        values = jnp.concatenate(values + [jnp.zeros((256 - used, 256), jnp.bfloat16)], axis=0)
        copies = jnp.dot(pick[plane], values, preferred_element_type=jnp.float32)
        copies = copies.astype(jnp.bfloat16)
        for shift in range(9):
            spread[pair, shift, plane] = copies[shift * PLANE : (shift + 1) * PLANE, :]

    def thin_rows(way, pair, count):
        return thin_in[PLACES[way][1]].astype(jnp.float32)[pair * count : (pair + 1) * count, :]

    def interact(levels):
        for sx in range(-3, 4):
            if levels[0] != 0:
                load_operators(sx).wait()
            for sy in range(-3, 4):
                weights, shifts = [], []
                for dz in (-1, 0, 1):
                    entries = [
                        [offsets.get((sx, sy, 2 * dz + cz - pz)) for pz in (0, 1)] for cz in (0, 1)
                    ]
                    if all(entry is None for row in entries for entry in row):
                        continue
                    blank = jnp.zeros((128, 128), jnp.bfloat16)
                    for row in entries:
                        row = [blank if entry is None else held[entry] for entry in row]
                        weights.append(jnp.concatenate(row, axis=1))
                    shifts.append(dz)
                weights = jnp.concatenate(weights, axis=0)
                classes, sources = [], []
                for px in (0, 1):
                    for py in (0, 1):
                        dx, cx = (px + sx) // 2, (px + sx) % 2
                        dy, cy = (py + sy) // 2, (py + sy) % 2
                        if abs(dx) > 1 or abs(dy) > 1:
                            continue
                        classes.append(px * 2 + py)
                        for z in levels:
                            planes = [
                                spread[cx * 2 + cy, (dy + 1) * 3 + dx + 1, 1 + z + dz] for dz in shifts
                            ]
                            sources.append(jnp.concatenate(planes, axis=1))
                product = jnp.dot(
                    jnp.concatenate(sources, axis=0), weights, preferred_element_type=jnp.float32
                )
                row = 0
                for kind in classes:
                    for z in levels:
                        total[kind, z] += product[row : row + PLANE, :]
                        row += PLANE

    total[...] = jnp.zeros_like(total)
    load_pick.wait()
    for way in ways:
        if way[2] == 0:
            arrive(way)
    for pair in range(4):
        lanes = slice(pair * 256, pair * 256 + 256)
        for corner, (ex, ey) in enumerate(PAIR_WAYS):
            rim[pair, corner * 4 : corner * 4 + 4, :] = thin_rows((ex, ey, 0), pair, 4)
        corners = rim[pair, 0:16, :].astype(jnp.bfloat16)
        for z in range(SIDE_Z):
            spread_plane(
                z + 1, pair, [own[z * PLANE : (z + 1) * PLANE, lanes], face_in[32:96, lanes], face_in[0:32, lanes], corners]
            )
    interact((1, 2))

    for way in ways:
        if way[2] != 0:
            arrive(way)
    for pair in range(4):
        lanes = slice(pair * 256, pair * 256 + 256)
        cx, cy = pair // 2, pair % 2
        for ez in (-1, 1):
            side = 4 + pair * 2 + (ez > 0)
            for number, ey in enumerate((-1, 1)):
                rows = edge_in[PLACES[(0, ey, ez)][1], :, cy * 256 : cy * 256 + 256].astype(jnp.float32)
                rim[side, number * 8 : number * 8 + 8, :] = rows[cx * 8 : cx * 8 + 8, :]
            for number, ex in enumerate((-1, 1)):
                rim[side, 16 + number * 4 : 20 + number * 4, :] = thin_rows((ex, 0, ez), pair, 4)
            for number, (ex, ey) in enumerate(PAIR_WAYS):
                rim[side, 24 + number : 25 + number, :] = thin_rows((ex, ey, ez), pair, 1)
            start = PLACES[(0, 0, ez)][1]
            spread_plane(
                0 if ez < 0 else SIDE_Z + 1, pair,
                [face_in[start : start + PLANE, lanes], rim[side].astype(jnp.bfloat16)],
            )
    interact((0, 3))

    for px in (0, 1):
        for py in (0, 1):
            for pz in (0, 1):
                rows = total[px * 2 + py, :, :, pz * 128 : pz * 128 + 128].reshape(PARENTS, 128)
                field[pl.ds(child_of(px, py, pz), PARENTS, stride=8), :] = rows
    for morton in range(0, PARENTS, 2):
        parts = [field[place * 8 : place * 8 + 8, :] for place in map(parent_place, (morton, morton + 1))]
        out[morton * 8 : morton * 8 + 16, :] = pack(parts)
    for way in ways:

        @pl.when(near[way][0])
        def _():
            copy_to(way).wait_send()


def expand_kernel(expand, reduced, out):
    out[...] = lax.dot_general(
        expand[...], reduced[...], (((1,), (1,)), ((), ())), preferred_element_type=jnp.float32
    )


def local(multipoles, compress, operators, expand):
    cells, rank = multipoles.shape[1], compress.shape[1]
    bit_lists = bits_of_dimension(lax.axis_size("cells"), cells.bit_length() - 1)
    vmem, anywhere = pl.BlockSpec(memory_space=pltpu.VMEM), pl.BlockSpec(memory_space=pl.ANY)
    table = jnp.asarray(picks(), jnp.bfloat16)
    half = jnp.bfloat16
    edges = sum(place[0] == "edge" for place in PLACES.values())
    thins = sum(place[0] == "thin" for place in PLACES.values())
    reduced = pl.pallas_call(
        functools.partial(reduce_kernel, bit_lists),
        out_shape=jax.ShapeDtypeStruct((cells, rank), half),
        in_specs=[anywhere] * 4,
        out_specs=vmem,
        scratch_shapes=[
            pltpu.VMEM(multipoles.shape, half),
            pltpu.VMEM(compress.shape, half),
            pltpu.VMEM(table.shape, half),
            pltpu.VMEM(operators.shape, half),
            pltpu.VMEM((cells, rank), jnp.float32),
            pltpu.VMEM((PARENTS, 8 * rank), half),
            pltpu.VMEM((96, 8 * rank), half),
            pltpu.VMEM((edges, 16, 4 * rank), half),
            pltpu.VMEM((thins, 16, 2 * rank), half),
            pltpu.VMEM((160, 8 * rank), half),
            pltpu.VMEM((edges, 16, 4 * rank), half),
            pltpu.VMEM((thins, 16, 2 * rank), half),
            pltpu.VMEM((12, 32, 2 * rank), jnp.float32),
            pltpu.VMEM((4, 9, SIDE_Z + 2, PLANE, 2 * rank), half),
            pltpu.VMEM((4, SIDE_Z, PLANE, 2 * rank), jnp.float32),
            pltpu.SemaphoreType.DMA((10,)),
            pltpu.SemaphoreType.DMA((len(WAYS),)),
            pltpu.SemaphoreType.DMA((len(WAYS),)),
        ],
        compiler_params=pltpu.CompilerParams(
            collective_id=0, has_side_effects=True, vmem_limit_bytes=48 * 2**20
        ),
        name="interactions",
    )(multipoles, compress, table, operators)
    return pl.pallas_call(
        expand_kernel,
        out_shape=jax.ShapeDtypeStruct((expand.shape[1], cells), jnp.float32),
        in_specs=[vmem] * 2,
        out_specs=vmem,
        compiler_params=pltpu.CompilerParams(vmem_limit_bytes=16 * 2**20),
        name="expansion",
    )(expand.T, reduced)


def solution(mesh):
    placed = (P(None, "cells"), P(), P(), P())
    return jax.shard_map(
        local, mesh=mesh, in_specs=placed, out_specs=P(None, "cells"), check_vma=False
    )
```

```python
import functools

import jax
import jax.numpy as jnp
import numpy as np
from jax import lax
from jax.experimental import pallas as pl
from jax.experimental.pallas import tpu as pltpu
from jax.sharding import PartitionSpec as P

SIDE_X, SIDE_Y, SIDE_Z = SIDE = (8, 4, 4)
PLANE = SIDE_X * SIDE_Y
PARENTS = PLANE * SIDE_Z
WAYS = [
    (ex, ey, ez)
    for ez in (0, -1, 1)
    for ey in (-1, 0, 1)
    for ex in (-1, 0, 1)
    if (ex, ey, ez) != (0, 0, 0)
]
PLACES = {
    (-1, 0, 0): ("face", 0, 16),
    (1, 0, 0): ("face", 16, 16),
    (0, -1, 0): ("face", 32, 32),
    (0, 1, 0): ("face", 64, 32),
    (0, 0, -1): ("face", 96, 32),
    (0, 0, 1): ("face", 128, 32),
}
for way in WAYS:
    if way not in PLACES:
        kind = "edge" if way[0] == 0 else "thin"
        PLACES[way] = (kind, sum(place[0] == kind for place in PLACES.values()), 16)
PAIR_WAYS = [(ex, ey) for ey in (-1, 1) for ex in (-1, 1)]


def offset_table():
    table = {}
    for sx in range(-3, 4):
        for sy in range(-3, 4):
            for sz in range(-3, 4):
                if max(abs(sx), abs(sy), abs(sz)) >= 2:
                    table[(sx, sy, sz)] = len(table)
    return table


def parent_place(morton):
    coords = [0, 0, 0]
    for bit in range(7):
        coords[bit % 3] += (morton >> bit & 1) << (bit // 3)
    return (coords[2] * SIDE_Y + coords[1]) * SIDE_X + coords[0]


def picks():
    table = np.zeros((SIDE_Z + 2, 9 * PLANE, 256), np.float32)
    for plane in range(SIDE_Z + 2):
        z = plane - 1
        outer = z < 0 or z >= SIDE_Z
        row = 0
        for dy in (-1, 0, 1):
            for dx in (-1, 0, 1):
                for y in range(SIDE_Y):
                    for x in range(SIDE_X):
                        sy, sx = y + dy, x + dx
                        ey = -1 if sy < 0 else 1 if sy >= SIDE_Y else 0
                        ex = -1 if sx < 0 else 1 if sx >= SIDE_X else 0
                        wy, wx = sy % SIDE_Y, sx % SIDE_X
                        if ex == 0 and ey == 0:
                            column = wy * SIDE_X + wx
                        elif ex == 0:
                            column = 32 + (ey > 0) * 8 + wx if outer else 32 + (ey > 0) * 32 + z * 8 + wx
                        elif ey == 0:
                            column = 48 + (ex > 0) * 4 + wy if outer else 96 + (ex > 0) * 16 + z * 4 + wy
                        else:
                            corner = PAIR_WAYS.index((ex, ey))
                            column = 56 + corner if outer else 128 + corner * 4 + z
                        table[plane, row, column] = 1
                        row += 1
    return table


def bits_of_dimension(device_count, local_bits):
    count = device_count.bit_length() - 1
    return [[bit for bit in range(count) if (local_bits + bit) % 3 == dim] for dim in range(3)]


def reduce_kernel(
    bit_lists, multipoles_hbm, compress_hbm, pick_hbm, operators, out,
    multipoles, compress, pick, held, field, own, face_out, edge_out, thin_out,
    face_in, edge_in, thin_in, rim, spread, total, load_sem, send_sem, recv_sem,
):
    offsets = offset_table()
    spans = {}
    for (sx, _, _), number in offsets.items():
        low, high = spans.get(sx, (number, number))
        spans[sx] = (min(low, number), max(high, number))

    def load_operators(sx):
        low, high = spans[sx]
        rows = pl.ds(low, high - low + 1)
        return pltpu.make_async_copy(operators.at[rows], held.at[rows], load_sem.at[sx + 6])

    load_multipoles = pltpu.make_async_copy(multipoles_hbm, multipoles, load_sem.at[0])
    load_compress = pltpu.make_async_copy(compress_hbm, compress, load_sem.at[1])
    load_pick = pltpu.make_async_copy(pick_hbm, pick, load_sem.at[2])
    load_multipoles.start()
    load_compress.start()
    load_pick.start()
    for sx in (-2, -1, 0, 1, 2, -3, 3):
        load_operators(sx).start()

    me = lax.axis_index("cells")
    position = []
    for bits in bit_lists:
        value = me * 0
        for rank, bit in enumerate(bits):
            value = value + (me // 2**bit) % 2 * 2**rank
        position.append(value)

    def neighbour(way):
        inside, device = None, me * 0
        for dim, bits in enumerate(bit_lists):
            place = position[dim] + way[dim]
            if way[dim]:
                fits = (place >= 0) & (place < 2 ** len(bits))
                inside = fits if inside is None else inside & fits
            for rank, bit in enumerate(bits):
                device = device + (place + 2 ** len(bits)) // 2**rank % 2 * 2**bit
        return inside, device

    ways = [way for way in WAYS if all(bits or not step for bits, step in zip(bit_lists, way))]
    near = {way: neighbour(way) for way in ways}
    barrier = pltpu.get_barrier_semaphore()
    peers = me * 0
    for way in ways:
        inside, device = near[way]
        peers = peers + jnp.where(inside, 1, 0)

        @pl.when(inside)
        def _():
            pl.semaphore_signal(barrier, inc=1, device_id=(device,), device_id_type=pl.DeviceIdType.MESH)

    def slot(buffers, way):
        kind, start, rows = PLACES[way]
        if kind == "face":
            return buffers[0].at[pl.ds(start, rows)]
        return buffers[1 if kind == "edge" else 2].at[start]

    inboxes = (face_in, edge_in, thin_in)
    for way in WAYS:
        target = slot(inboxes, way)
        if way in near:

            @pl.when(jnp.logical_not(near[way][0]))
            def _():
                target[...] = jnp.zeros(target.shape, target.dtype)
        else:
            target[...] = jnp.zeros(target.shape, target.dtype)
    rim[...] = jnp.zeros_like(rim)

    load_multipoles.wait()
    load_compress.wait()
    compressed = lax.dot_general(
        multipoles[...], compress[...], (((0,), (0,)), ((), ())), preferred_element_type=jnp.float32
    )
    compressed = compressed.astype(jnp.bfloat16).astype(jnp.float32)
    for morton in range(PARENTS):
        place = parent_place(morton)
        field[place * 8 : place * 8 + 8, :] = compressed[morton * 8 : morton * 8 + 8, :]

    def child_of(cx, cy, cz):
        return cx + 2 * cy + 4 * cz

    def line(place, child, count, step):
        return field[pl.ds(place * 8 + child, count, stride=step * 8), :]

    def pack(parts):
        return jnp.concatenate(parts, axis=0).astype(jnp.bfloat16)

    children = [(cx, cy, cz) for cx in (0, 1) for cy in (0, 1) for cz in (0, 1)]
    for number, bits in enumerate(children):
        child, lanes = child_of(*bits), slice(number * 128, number * 128 + 128)
        for z in range(SIDE_Z):
            own[z * PLANE : (z + 1) * PLANE, lanes] = line(z * PLANE, child, PLANE, 1).astype(jnp.bfloat16)
        for ex in (-1, 1):
            start = PLACES[(ex, 0, 0)][1]
            x = SIDE_X - 1 if ex > 0 else 0
            face_out[start : start + 16, lanes] = line(x, child, 16, SIDE_X).astype(jnp.bfloat16)
        for ey in (-1, 1):
            start = PLACES[(0, ey, 0)][1]
            y = SIDE_Y - 1 if ey > 0 else 0
            parts = [line(z * PLANE + y * SIDE_X, child, SIDE_X, 1) for z in range(SIDE_Z)]
            face_out[start : start + 32, lanes] = pack(parts)
    for way in WAYS:
        kind, start, _ = PLACES[way]
        x = SIDE_X - 1 if way[0] > 0 else 0
        y = SIDE_Y - 1 if way[1] > 0 else 0
        z = SIDE_Z - 1 if way[2] > 0 else 0
        place = z * PLANE + y * SIDE_X + x
        if kind == "edge":
            for cy in (0, 1):
                for cz in (0, 1):
                    parts = [line(place, child_of(cx, cy, cz), SIDE_X, 1) for cx in (0, 1)]
                    edge_out[start, :, (cy * 2 + cz) * 128 : (cy * 2 + cz + 1) * 128] = pack(parts)
        elif kind == "thin":
            for cz in (0, 1):
                parts = []
                for pair in range(4):
                    child = child_of(pair // 2, pair % 2, cz)
                    if way[2] == 0:
                        parts.append(line(place, child, SIDE_Z, PLANE))
                    elif way[1] == 0:
                        parts.append(line(place, child, SIDE_Y, SIDE_X))
                    else:
                        parts.append(field[place * 8 + child : place * 8 + child + 1, :])
                if way[1] and way[2]:
                    parts.append(jnp.zeros((12, 128), jnp.float32))
                thin_out[start, :, cz * 128 : cz * 128 + 128] = pack(parts)

    pl.semaphore_wait(barrier, peers)

    def copy_to(way):
        back = tuple(-step for step in way)
        if way[:2] == (0, 0):
            source = own.at[pl.ds(PARENTS - PLANE if way[2] > 0 else 0, PLANE)]
        else:
            source = slot((face_out, edge_out, thin_out), way)
        return pltpu.make_async_remote_copy(
            src_ref=source,
            dst_ref=slot(inboxes, back),
            send_sem=send_sem.at[WAYS.index(way)],
            recv_sem=recv_sem.at[WAYS.index(back)],
            device_id=(near[way][1],),
            device_id_type=pl.DeviceIdType.MESH,
        )

    for way in ways:

        @pl.when(near[way][0])
        def _():
            copy_to(way).start()

    def arrive(way):
        @pl.when(near[way][0])
        def _():
            copy_to(tuple(-step for step in way)).wait_recv()

    def spread_plane(plane, pair, values):
        used = sum(value.shape[0] for value in values)
        values = jnp.concatenate(values + [jnp.zeros((256 - used, 256), jnp.bfloat16)], axis=0)
        copies = jnp.dot(pick[plane], values, preferred_element_type=jnp.float32)
        copies = copies.astype(jnp.bfloat16)
        for shift in range(9):
            spread[pair, shift, plane] = copies[shift * PLANE : (shift + 1) * PLANE, :]

    def thin_rows(way, pair, count):
        return thin_in[PLACES[way][1]].astype(jnp.float32)[pair * count : (pair + 1) * count, :]

    def weights_of(sx, sy):
        weights, shifts = [], []
        for dz in (-1, 0, 1):
            entries = [[offsets.get((sx, sy, 2 * dz + cz - pz)) for pz in (0, 1)] for cz in (0, 1)]
            if all(entry is None for row in entries for entry in row):
                continue
            blank = jnp.zeros((128, 128), jnp.bfloat16)
            for row in entries:
                row = [blank if entry is None else held[entry] for entry in row]
                weights.append(jnp.concatenate(row, axis=1))
            shifts.append(dz)
        return weights, shifts

    def interact(levels, group):
        sx, sy = group[0]
        classes = [
            (px, py)
            for px in (0, 1)
            for py in (0, 1)
            if abs((px + sx) // 2) <= 1 and abs((py + sy) // 2) <= 1
        ]
        weights, sources = [], {(kind, z): [] for kind in classes for z in levels}
        for sx, sy in group:
            tiles, shifts = weights_of(sx, sy)
            weights += tiles
            for px, py in classes:
                dx, cx = (px + sx) // 2, (px + sx) % 2
                dy, cy = (py + sy) // 2, (py + sy) % 2
                for z in levels:
                    for dz in shifts:
                        plane = spread[cx * 2 + cy, (dy + 1) * 3 + dx + 1, 1 + z + dz]
                        sources[(px, py), z].append(plane)
        rows = [jnp.concatenate(planes, axis=1) for planes in sources.values()]
        product = jnp.dot(
            jnp.concatenate(rows, axis=0),
            jnp.concatenate(weights, axis=0),
            preferred_element_type=jnp.float32,
        )
        for number, ((px, py), z) in enumerate(sources):
            total[px * 2 + py, z] += product[number * PLANE : (number + 1) * PLANE, :]

    middle = range(-2, 3)

    total[...] = jnp.zeros_like(total)
    load_pick.wait()
    for way in ways:
        if way[2] == 0:
            arrive(way)
    for pair in range(4):
        lanes = slice(pair * 256, pair * 256 + 256)
        for corner, (ex, ey) in enumerate(PAIR_WAYS):
            rim[pair, corner * 4 : corner * 4 + 4, :] = thin_rows((ex, ey, 0), pair, 4)
        corners = rim[pair, 0:16, :].astype(jnp.bfloat16)
        for z in range(SIDE_Z):
            spread_plane(
                z + 1, pair, [own[z * PLANE : (z + 1) * PLANE, lanes], face_in[32:96, lanes], face_in[0:32, lanes], corners]
            )
    for sx in middle:
        load_operators(sx).wait()
        interact((1, 2), [(sx, sy) for sy in middle])

    for way in ways:
        if way[2] != 0:
            arrive(way)
    for pair in range(4):
        lanes = slice(pair * 256, pair * 256 + 256)
        cx, cy = pair // 2, pair % 2
        for ez in (-1, 1):
            side = 4 + pair * 2 + (ez > 0)
            for number, ey in enumerate((-1, 1)):
                rows = edge_in[PLACES[(0, ey, ez)][1], :, cy * 256 : cy * 256 + 256].astype(jnp.float32)
                rim[side, number * 8 : number * 8 + 8, :] = rows[cx * 8 : cx * 8 + 8, :]
            for number, ex in enumerate((-1, 1)):
                rim[side, 16 + number * 4 : 20 + number * 4, :] = thin_rows((ex, 0, ez), pair, 4)
            for number, (ex, ey) in enumerate(PAIR_WAYS):
                rim[side, 24 + number : 25 + number, :] = thin_rows((ex, ey, ez), pair, 1)
            start = PLACES[(0, 0, ez)][1]
            spread_plane(
                0 if ez < 0 else SIDE_Z + 1, pair,
                [face_in[start : start + PLANE, lanes], rim[side].astype(jnp.bfloat16)],
            )
    for sx in middle:
        interact((0, 3), [(sx, sy) for sy in middle])
    levels = range(SIDE_Z)
    for sx in (-3, 3):
        load_operators(sx).wait()
    for far in (-3, 3):
        interact(levels, [(far, sy) for sy in middle])
        interact(levels, [(sx, far) for sx in middle])
        for other in (-3, 3):
            interact(levels, [(far, other)])

    for px in (0, 1):
        for py in (0, 1):
            for pz in (0, 1):
                rows = total[px * 2 + py, :, :, pz * 128 : pz * 128 + 128].reshape(PARENTS, 128)
                field[pl.ds(child_of(px, py, pz), PARENTS, stride=8), :] = rows
    for morton in range(0, PARENTS, 2):
        parts = [field[place * 8 : place * 8 + 8, :] for place in map(parent_place, (morton, morton + 1))]
        out[morton * 8 : morton * 8 + 16, :] = pack(parts)
    for way in ways:

        @pl.when(near[way][0])
        def _():
            copy_to(way).wait_send()


def expand_kernel(expand, reduced, out):
    out[...] = lax.dot_general(
        expand[...], reduced[...], (((1,), (1,)), ((), ())), preferred_element_type=jnp.float32
    )


def local(multipoles, compress, operators, expand):
    cells, rank = multipoles.shape[1], compress.shape[1]
    bit_lists = bits_of_dimension(lax.axis_size("cells"), cells.bit_length() - 1)
    vmem, anywhere = pl.BlockSpec(memory_space=pltpu.VMEM), pl.BlockSpec(memory_space=pl.ANY)
    table = jnp.asarray(picks(), jnp.bfloat16)
    half = jnp.bfloat16
    edges = sum(place[0] == "edge" for place in PLACES.values())
    thins = sum(place[0] == "thin" for place in PLACES.values())
    reduced = pl.pallas_call(
        functools.partial(reduce_kernel, bit_lists),
        out_shape=jax.ShapeDtypeStruct((cells, rank), half),
        in_specs=[anywhere] * 4,
        out_specs=vmem,
        scratch_shapes=[
            pltpu.VMEM(multipoles.shape, half),
            pltpu.VMEM(compress.shape, half),
            pltpu.VMEM(table.shape, half),
            pltpu.VMEM(operators.shape, half),
            pltpu.VMEM((cells, rank), jnp.float32),
            pltpu.VMEM((PARENTS, 8 * rank), half),
            pltpu.VMEM((96, 8 * rank), half),
            pltpu.VMEM((edges, 16, 4 * rank), half),
            pltpu.VMEM((thins, 16, 2 * rank), half),
            pltpu.VMEM((160, 8 * rank), half),
            pltpu.VMEM((edges, 16, 4 * rank), half),
            pltpu.VMEM((thins, 16, 2 * rank), half),
            pltpu.VMEM((12, 32, 2 * rank), jnp.float32),
            pltpu.VMEM((4, 9, SIDE_Z + 2, PLANE, 2 * rank), half),
            pltpu.VMEM((4, SIDE_Z, PLANE, 2 * rank), jnp.float32),
            pltpu.SemaphoreType.DMA((10,)),
            pltpu.SemaphoreType.DMA((len(WAYS),)),
            pltpu.SemaphoreType.DMA((len(WAYS),)),
        ],
        compiler_params=pltpu.CompilerParams(
            collective_id=0, has_side_effects=True, vmem_limit_bytes=62 * 2**20
        ),
        name="interactions",
    )(multipoles, compress, table, operators)
    return pl.pallas_call(
        expand_kernel,
        out_shape=jax.ShapeDtypeStruct((expand.shape[1], cells), jnp.float32),
        in_specs=[vmem] * 2,
        out_specs=vmem,
        compiler_params=pltpu.CompilerParams(vmem_limit_bytes=16 * 2**20),
        name="expansion",
    )(expand.T, reduced)


def solution(mesh):
    placed = (P(None, "cells"), P(), P(), P())
    return jax.shard_map(
        local, mesh=mesh, in_specs=placed, out_specs=P(None, "cells"), check_vma=False
    )
```

```python
import functools

import jax
import jax.numpy as jnp
import numpy as np
from jax import lax
from jax.experimental import pallas as pl
from jax.experimental.pallas import tpu as pltpu
from jax.sharding import PartitionSpec as P

SIDE_X, SIDE_Y, SIDE_Z = SIDE = (8, 4, 4)
PLANE = SIDE_X * SIDE_Y
PARENTS = PLANE * SIDE_Z
WAYS = [
    (ex, ey, ez)
    for ez in (0, -1, 1)
    for ey in (-1, 0, 1)
    for ex in (-1, 0, 1)
    if (ex, ey, ez) != (0, 0, 0)
]
PLACES = {
    (-1, 0, 0): ("face", 0, 16),
    (1, 0, 0): ("face", 16, 16),
    (0, -1, 0): ("face", 32, 32),
    (0, 1, 0): ("face", 64, 32),
    (0, 0, -1): ("face", 96, 32),
    (0, 0, 1): ("face", 128, 32),
}
for way in WAYS:
    if way not in PLACES:
        kind = "edge" if way[0] == 0 else "thin"
        PLACES[way] = (kind, sum(place[0] == kind for place in PLACES.values()), 16)
PAIR_WAYS = [(ex, ey) for ey in (-1, 1) for ex in (-1, 1)]


def offset_table():
    table = {}
    for sx in range(-3, 4):
        for sy in range(-3, 4):
            for sz in range(-3, 4):
                if max(abs(sx), abs(sy), abs(sz)) >= 2:
                    table[(sx, sy, sz)] = len(table)
    return table


def parent_place(morton):
    coords = [0, 0, 0]
    for bit in range(7):
        coords[bit % 3] += (morton >> bit & 1) << (bit // 3)
    return (coords[2] * SIDE_Y + coords[1]) * SIDE_X + coords[0]


def picks():
    table = np.zeros((SIDE_Z + 2, 9 * PLANE, 256), np.float32)
    for plane in range(SIDE_Z + 2):
        z = plane - 1
        outer = z < 0 or z >= SIDE_Z
        row = 0
        for dy in (-1, 0, 1):
            for dx in (-1, 0, 1):
                for y in range(SIDE_Y):
                    for x in range(SIDE_X):
                        sy, sx = y + dy, x + dx
                        ey = -1 if sy < 0 else 1 if sy >= SIDE_Y else 0
                        ex = -1 if sx < 0 else 1 if sx >= SIDE_X else 0
                        wy, wx = sy % SIDE_Y, sx % SIDE_X
                        if ex == 0 and ey == 0:
                            column = wy * SIDE_X + wx
                        elif ex == 0:
                            column = 32 + (ey > 0) * 8 + wx if outer else 32 + (ey > 0) * 32 + z * 8 + wx
                        elif ey == 0:
                            column = 48 + (ex > 0) * 4 + wy if outer else 96 + (ex > 0) * 16 + z * 4 + wy
                        else:
                            corner = PAIR_WAYS.index((ex, ey))
                            column = 56 + corner if outer else 128 + corner * 4 + z
                        table[plane, row, column] = 1
                        row += 1
    return table


def bits_of_dimension(device_count, local_bits):
    count = device_count.bit_length() - 1
    return [[bit for bit in range(count) if (local_bits + bit) % 3 == dim] for dim in range(3)]


def reduce_kernel(
    bit_lists, multipoles_hbm, compress_hbm, pick_hbm, operators, out,
    multipoles, compress, pick, held, field, own, face_out, edge_out, thin_out,
    face_in, edge_in, thin_in, rim, spread, total, load_sem, send_sem, recv_sem,
):
    offsets = offset_table()
    spans = {}
    for (sx, _, _), number in offsets.items():
        low, high = spans.get(sx, (number, number))
        spans[sx] = (min(low, number), max(high, number))

    def load_operators(sx):
        low, high = spans[sx]
        rows = pl.ds(low, high - low + 1)
        return pltpu.make_async_copy(operators.at[rows], held.at[rows], load_sem.at[sx + 6])

    load_multipoles = pltpu.make_async_copy(multipoles_hbm, multipoles, load_sem.at[0])
    load_compress = pltpu.make_async_copy(compress_hbm, compress, load_sem.at[1])
    load_pick = pltpu.make_async_copy(pick_hbm, pick, load_sem.at[2])
    load_multipoles.start()
    load_compress.start()
    load_pick.start()
    for sx in (-2, -1, 0, 1, 2, -3, 3):
        load_operators(sx).start()

    me = lax.axis_index("cells")
    position = []
    for bits in bit_lists:
        value = me * 0
        for rank, bit in enumerate(bits):
            value = value + (me // 2**bit) % 2 * 2**rank
        position.append(value)

    def neighbour(way):
        inside, device = None, me * 0
        for dim, bits in enumerate(bit_lists):
            place = position[dim] + way[dim]
            if way[dim]:
                fits = (place >= 0) & (place < 2 ** len(bits))
                inside = fits if inside is None else inside & fits
            for rank, bit in enumerate(bits):
                device = device + (place + 2 ** len(bits)) // 2**rank % 2 * 2**bit
        return inside, device

    ways = [way for way in WAYS if all(bits or not step for bits, step in zip(bit_lists, way))]
    near = {way: neighbour(way) for way in ways}
    barrier = pltpu.get_barrier_semaphore()
    peers = me * 0
    for way in ways:
        inside, device = near[way]
        peers = peers + jnp.where(inside, 1, 0)

        @pl.when(inside)
        def _():
            pl.semaphore_signal(barrier, inc=1, device_id=(device,), device_id_type=pl.DeviceIdType.MESH)

    def slot(buffers, way):
        kind, start, rows = PLACES[way]
        if kind == "face":
            return buffers[0].at[pl.ds(start, rows)]
        return buffers[1 if kind == "edge" else 2].at[start]

    inboxes = (face_in, edge_in, thin_in)
    for way in WAYS:
        target = slot(inboxes, way)
        if way in near:

            @pl.when(jnp.logical_not(near[way][0]))
            def _():
                target[...] = jnp.zeros(target.shape, target.dtype)
        else:
            target[...] = jnp.zeros(target.shape, target.dtype)
    rim[...] = jnp.zeros_like(rim)

    load_multipoles.wait()
    load_compress.wait()
    compressed = lax.dot_general(
        multipoles[...], compress[...], (((0,), (0,)), ((), ())), preferred_element_type=jnp.float32
    )
    compressed = compressed.astype(jnp.bfloat16).astype(jnp.float32)
    for morton in range(PARENTS):
        place = parent_place(morton)
        field[place * 8 : place * 8 + 8, :] = compressed[morton * 8 : morton * 8 + 8, :]

    def child_of(cx, cy, cz):
        return cx + 2 * cy + 4 * cz

    def line(place, child, count, step):
        return field[pl.ds(place * 8 + child, count, stride=step * 8), :]

    def pack(parts):
        return jnp.concatenate(parts, axis=0).astype(jnp.bfloat16)

    children = [(cx, cy, cz) for cx in (0, 1) for cy in (0, 1) for cz in (0, 1)]

    def pack_own(z):
        for number, bits in enumerate(children):
            rows = line(z * PLANE, child_of(*bits), PLANE, 1)
            own[z * PLANE : (z + 1) * PLANE, number * 128 : number * 128 + 128] = rows.astype(jnp.bfloat16)

    def pack_way(way):
        kind, start, rows = PLACES[way]
        x = SIDE_X - 1 if way[0] > 0 else 0
        y = SIDE_Y - 1 if way[1] > 0 else 0
        z = SIDE_Z - 1 if way[2] > 0 else 0
        place = z * PLANE + y * SIDE_X + x
        if kind == "face":
            for number, bits in enumerate(children):
                child = child_of(*bits)
                if way[0]:
                    parts = [line(x, child, 16, SIDE_X)]
                else:
                    parts = [line(z * PLANE + y * SIDE_X, child, SIDE_X, 1) for z in range(SIDE_Z)]
                face_out[start : start + rows, number * 128 : number * 128 + 128] = pack(parts)
        elif kind == "edge":
            for cy in (0, 1):
                for cz in (0, 1):
                    parts = [line(place, child_of(cx, cy, cz), SIDE_X, 1) for cx in (0, 1)]
                    edge_out[start, :, (cy * 2 + cz) * 128 : (cy * 2 + cz + 1) * 128] = pack(parts)
        else:
            for cz in (0, 1):
                parts = []
                for pair in range(4):
                    child = child_of(pair // 2, pair % 2, cz)
                    if way[2] == 0:
                        parts.append(line(place, child, SIDE_Z, PLANE))
                    elif way[1] == 0:
                        parts.append(line(place, child, SIDE_Y, SIDE_X))
                    else:
                        parts.append(field[place * 8 + child : place * 8 + child + 1, :])
                if way[1] and way[2]:
                    parts.append(jnp.zeros((12, 128), jnp.float32))
                thin_out[start, :, cz * 128 : cz * 128 + 128] = pack(parts)

    def copy_to(way):
        back = tuple(-step for step in way)
        if way[:2] == (0, 0):
            source = own.at[pl.ds(PARENTS - PLANE if way[2] > 0 else 0, PLANE)]
        else:
            source = slot((face_out, edge_out, thin_out), way)
        return pltpu.make_async_remote_copy(
            src_ref=source,
            dst_ref=slot(inboxes, back),
            send_sem=send_sem.at[WAYS.index(way)],
            recv_sem=recv_sem.at[WAYS.index(back)],
            device_id=(near[way][1],),
            device_id_type=pl.DeviceIdType.MESH,
        )

    def send(some):
        for way in some:

            @pl.when(near[way][0])
            def _():
                copy_to(way).start()

    flat_ways = [way for way in ways if way[2] == 0]
    face_ways = [way for way in ways if way[:2] == (0, 0)]
    slant_ways = [way for way in ways if way[2] != 0 and way not in face_ways]
    for way in flat_ways:
        pack_way(way)
    pl.semaphore_wait(barrier, peers)
    send(flat_ways)
    pack_own(0)
    pack_own(SIDE_Z - 1)
    send(face_ways)
    for way in slant_ways:
        pack_way(way)
    send(slant_ways)
    for z in range(1, SIDE_Z - 1):
        pack_own(z)

    def arrive(way):
        @pl.when(near[way][0])
        def _():
            copy_to(tuple(-step for step in way)).wait_recv()

    def spread_plane(plane, pair, values):
        used = sum(value.shape[0] for value in values)
        values = jnp.concatenate(values + [jnp.zeros((256 - used, 256), jnp.bfloat16)], axis=0)
        copies = jnp.dot(pick[plane], values, preferred_element_type=jnp.float32)
        copies = copies.astype(jnp.bfloat16)
        for shift in range(9):
            spread[pair, shift, plane] = copies[shift * PLANE : (shift + 1) * PLANE, :]

    def thin_rows(way, pair, count):
        return thin_in[PLACES[way][1]].astype(jnp.float32)[pair * count : (pair + 1) * count, :]

    def weights_of(sx, sy):
        weights, shifts = [], []
        for dz in (-1, 0, 1):
            entries = [[offsets.get((sx, sy, 2 * dz + cz - pz)) for pz in (0, 1)] for cz in (0, 1)]
            if all(entry is None for row in entries for entry in row):
                continue
            blank = jnp.zeros((128, 128), jnp.bfloat16)
            for row in entries:
                row = [blank if entry is None else held[entry] for entry in row]
                weights.append(jnp.concatenate(row, axis=1))
            shifts.append(dz)
        return weights, shifts

    def interact(levels, group):
        sx, sy = group[0]
        classes = [
            (px, py)
            for px in (0, 1)
            for py in (0, 1)
            if abs((px + sx) // 2) <= 1 and abs((py + sy) // 2) <= 1
        ]
        weights, sources = [], {(kind, z): [] for kind in classes for z in levels}
        for sx, sy in group:
            tiles, shifts = weights_of(sx, sy)
            weights += tiles
            for px, py in classes:
                dx, cx = (px + sx) // 2, (px + sx) % 2
                dy, cy = (py + sy) // 2, (py + sy) % 2
                for z in levels:
                    for dz in shifts:
                        plane = spread[cx * 2 + cy, (dy + 1) * 3 + dx + 1, 1 + z + dz]
                        sources[(px, py), z].append(plane)
        rows = [jnp.concatenate(planes, axis=1) for planes in sources.values()]
        product = jnp.dot(
            jnp.concatenate(rows, axis=0),
            jnp.concatenate(weights, axis=0),
            preferred_element_type=jnp.float32,
        )
        for number, ((px, py), z) in enumerate(sources):
            total[px * 2 + py, z] += product[number * PLANE : (number + 1) * PLANE, :]

    middle = range(-2, 3)

    total[...] = jnp.zeros_like(total)
    load_pick.wait()
    for way in ways:
        if way[2] == 0:
            arrive(way)
    for pair in range(4):
        lanes = slice(pair * 256, pair * 256 + 256)
        for corner, (ex, ey) in enumerate(PAIR_WAYS):
            rim[pair, corner * 4 : corner * 4 + 4, :] = thin_rows((ex, ey, 0), pair, 4)
        corners = rim[pair, 0:16, :].astype(jnp.bfloat16)
        for z in range(SIDE_Z):
            spread_plane(
                z + 1, pair, [own[z * PLANE : (z + 1) * PLANE, lanes], face_in[32:96, lanes], face_in[0:32, lanes], corners]
            )
    for sx in middle:
        load_operators(sx).wait()
        interact((1, 2), [(sx, sy) for sy in middle])

    for way in ways:
        if way[2] != 0:
            arrive(way)
    for pair in range(4):
        lanes = slice(pair * 256, pair * 256 + 256)
        cx, cy = pair // 2, pair % 2
        for ez in (-1, 1):
            side = 4 + pair * 2 + (ez > 0)
            for number, ey in enumerate((-1, 1)):
                rows = edge_in[PLACES[(0, ey, ez)][1], :, cy * 256 : cy * 256 + 256].astype(jnp.float32)
                rim[side, number * 8 : number * 8 + 8, :] = rows[cx * 8 : cx * 8 + 8, :]
            for number, ex in enumerate((-1, 1)):
                rim[side, 16 + number * 4 : 20 + number * 4, :] = thin_rows((ex, 0, ez), pair, 4)
            for number, (ex, ey) in enumerate(PAIR_WAYS):
                rim[side, 24 + number : 25 + number, :] = thin_rows((ex, ey, ez), pair, 1)
            start = PLACES[(0, 0, ez)][1]
            spread_plane(
                0 if ez < 0 else SIDE_Z + 1, pair,
                [face_in[start : start + PLANE, lanes], rim[side].astype(jnp.bfloat16)],
            )
    for sx in middle:
        interact((0, 3), [(sx, sy) for sy in middle])
    levels = range(SIDE_Z)
    for sx in (-3, 3):
        load_operators(sx).wait()
    for far in (-3, 3):
        interact(levels, [(far, sy) for sy in middle])
        interact(levels, [(sx, far) for sx in middle])
        for other in (-3, 3):
            interact(levels, [(far, other)])

    for px in (0, 1):
        for py in (0, 1):
            for pz in (0, 1):
                rows = total[px * 2 + py, :, :, pz * 128 : pz * 128 + 128].reshape(PARENTS, 128)
                field[pl.ds(child_of(px, py, pz), PARENTS, stride=8), :] = rows
    for morton in range(0, PARENTS, 2):
        parts = [field[place * 8 : place * 8 + 8, :] for place in map(parent_place, (morton, morton + 1))]
        out[morton * 8 : morton * 8 + 16, :] = pack(parts)
    for way in ways:

        @pl.when(near[way][0])
        def _():
            copy_to(way).wait_send()


def expand_kernel(expand, reduced, out):
    out[...] = lax.dot_general(
        expand[...], reduced[...], (((1,), (1,)), ((), ())), preferred_element_type=jnp.float32
    )


def local(multipoles, compress, operators, expand):
    cells, rank = multipoles.shape[1], compress.shape[1]
    bit_lists = bits_of_dimension(lax.axis_size("cells"), cells.bit_length() - 1)
    vmem, anywhere = pl.BlockSpec(memory_space=pltpu.VMEM), pl.BlockSpec(memory_space=pl.ANY)
    table = jnp.asarray(picks(), jnp.bfloat16)
    half = jnp.bfloat16
    edges = sum(place[0] == "edge" for place in PLACES.values())
    thins = sum(place[0] == "thin" for place in PLACES.values())
    reduced = pl.pallas_call(
        functools.partial(reduce_kernel, bit_lists),
        out_shape=jax.ShapeDtypeStruct((cells, rank), half),
        in_specs=[anywhere] * 4,
        out_specs=vmem,
        scratch_shapes=[
            pltpu.VMEM(multipoles.shape, half),
            pltpu.VMEM(compress.shape, half),
            pltpu.VMEM(table.shape, half),
            pltpu.VMEM(operators.shape, half),
            pltpu.VMEM((cells, rank), jnp.float32),
            pltpu.VMEM((PARENTS, 8 * rank), half),
            pltpu.VMEM((96, 8 * rank), half),
            pltpu.VMEM((edges, 16, 4 * rank), half),
            pltpu.VMEM((thins, 16, 2 * rank), half),
            pltpu.VMEM((160, 8 * rank), half),
            pltpu.VMEM((edges, 16, 4 * rank), half),
            pltpu.VMEM((thins, 16, 2 * rank), half),
            pltpu.VMEM((12, 32, 2 * rank), jnp.float32),
            pltpu.VMEM((4, 9, SIDE_Z + 2, PLANE, 2 * rank), half),
            pltpu.VMEM((4, SIDE_Z, PLANE, 2 * rank), jnp.float32),
            pltpu.SemaphoreType.DMA((10,)),
            pltpu.SemaphoreType.DMA((len(WAYS),)),
            pltpu.SemaphoreType.DMA((len(WAYS),)),
        ],
        compiler_params=pltpu.CompilerParams(
            collective_id=0, has_side_effects=True, vmem_limit_bytes=62 * 2**20
        ),
        name="interactions",
    )(multipoles, compress, table, operators)
    columns = cells // 2
    return pl.pallas_call(
        expand_kernel,
        out_shape=jax.ShapeDtypeStruct((expand.shape[1], cells), jnp.float32),
        grid=(cells // columns,),
        in_specs=[
            pl.BlockSpec((expand.shape[1], rank), lambda step: (0, 0)),
            pl.BlockSpec((columns, rank), lambda step: (step, 0)),
        ],
        out_specs=pl.BlockSpec((expand.shape[1], columns), lambda step: (0, step)),
        compiler_params=pltpu.CompilerParams(vmem_limit_bytes=62 * 2**20),
        name="expansion",
    )(expand.T, reduced)


def solution(mesh):
    placed = (P(None, "cells"), P(), P(), P())
    return jax.shard_map(
        local, mesh=mesh, in_specs=placed, out_specs=P(None, "cells"), check_vma=False
    )
```

```python
import functools

import jax
import jax.numpy as jnp
import numpy as np
from jax import lax
from jax.experimental import pallas as pl
from jax.experimental.pallas import tpu as pltpu
from jax.sharding import PartitionSpec as P

SIDE_X, SIDE_Y, SIDE_Z = SIDE = (8, 4, 4)
PLANE = SIDE_X * SIDE_Y
PARENTS = PLANE * SIDE_Z
WAYS = [
    (ex, ey, ez)
    for ez in (0, -1, 1)
    for ey in (-1, 0, 1)
    for ex in (-1, 0, 1)
    if (ex, ey, ez) != (0, 0, 0)
]
PLACES = {
    (-1, 0, 0): ("face", 0, 16),
    (1, 0, 0): ("face", 16, 16),
    (0, -1, 0): ("face", 32, 32),
    (0, 1, 0): ("face", 64, 32),
    (0, 0, -1): ("face", 96, 32),
    (0, 0, 1): ("face", 128, 32),
}
for way in WAYS:
    if way not in PLACES:
        kind = "edge" if way[0] == 0 else "thin"
        PLACES[way] = (kind, sum(place[0] == kind for place in PLACES.values()), 16)
PAIR_WAYS = [(ex, ey) for ey in (-1, 1) for ex in (-1, 1)]


def offset_table():
    table = {}
    for sx in range(-3, 4):
        for sy in range(-3, 4):
            for sz in range(-3, 4):
                if max(abs(sx), abs(sy), abs(sz)) >= 2:
                    table[(sx, sy, sz)] = len(table)
    return table


def parent_place(morton):
    coords = [0, 0, 0]
    for bit in range(7):
        coords[bit % 3] += (morton >> bit & 1) << (bit // 3)
    return (coords[2] * SIDE_Y + coords[1]) * SIDE_X + coords[0]


def picks():
    table = np.zeros((SIDE_Z + 2, 9 * PLANE, 256), np.float32)
    for plane in range(SIDE_Z + 2):
        z = plane - 1
        outer = z < 0 or z >= SIDE_Z
        row = 0
        for dy in (-1, 0, 1):
            for dx in (-1, 0, 1):
                for y in range(SIDE_Y):
                    for x in range(SIDE_X):
                        sy, sx = y + dy, x + dx
                        ey = -1 if sy < 0 else 1 if sy >= SIDE_Y else 0
                        ex = -1 if sx < 0 else 1 if sx >= SIDE_X else 0
                        wy, wx = sy % SIDE_Y, sx % SIDE_X
                        if ex == 0 and ey == 0:
                            column = wy * SIDE_X + wx
                        elif ex == 0:
                            column = 32 + (ey > 0) * 8 + wx if outer else 32 + (ey > 0) * 32 + z * 8 + wx
                        elif ey == 0:
                            column = 48 + (ex > 0) * 4 + wy if outer else 96 + (ex > 0) * 16 + z * 4 + wy
                        else:
                            corner = PAIR_WAYS.index((ex, ey))
                            column = 56 + corner if outer else 128 + corner * 4 + z
                        table[plane, row, column] = 1
                        row += 1
    return table


def bits_of_dimension(device_count, local_bits):
    count = device_count.bit_length() - 1
    return [[bit for bit in range(count) if (local_bits + bit) % 3 == dim] for dim in range(3)]


def reduce_kernel(
    bit_lists, multipoles_hbm, compress_hbm, pick_hbm, operators, out,
    multipoles, compress, pick, held, field, own, face_out, edge_out, thin_out,
    face_in, edge_in, thin_in, rim, spread, total, load_sem, send_sem, recv_sem,
):
    offsets = offset_table()
    spans = {}
    for (sx, _, _), number in offsets.items():
        low, high = spans.get(sx, (number, number))
        spans[sx] = (min(low, number), max(high, number))

    def load_operators(sx):
        low, high = spans[sx]
        rows = pl.ds(low, high - low + 1)
        return pltpu.make_async_copy(operators.at[rows], held.at[rows], load_sem.at[sx + 6])

    load_multipoles = pltpu.make_async_copy(multipoles_hbm, multipoles, load_sem.at[0])
    load_compress = pltpu.make_async_copy(compress_hbm, compress, load_sem.at[1])
    load_pick = pltpu.make_async_copy(pick_hbm, pick, load_sem.at[2])
    load_multipoles.start()
    load_compress.start()
    load_pick.start()
    for sx in (-2, -1, 0, 1, 2, -3, 3):
        load_operators(sx).start()

    me = lax.axis_index("cells")
    position = []
    for bits in bit_lists:
        value = me * 0
        for rank, bit in enumerate(bits):
            value = value + (me // 2**bit) % 2 * 2**rank
        position.append(value)

    def neighbour(way):
        inside, device = None, me * 0
        for dim, bits in enumerate(bit_lists):
            place = position[dim] + way[dim]
            if way[dim]:
                fits = (place >= 0) & (place < 2 ** len(bits))
                inside = fits if inside is None else inside & fits
            for rank, bit in enumerate(bits):
                device = device + (place + 2 ** len(bits)) // 2**rank % 2 * 2**bit
        return inside, device

    ways = [way for way in WAYS if all(bits or not step for bits, step in zip(bit_lists, way))]
    near = {way: neighbour(way) for way in ways}
    barrier = pltpu.get_barrier_semaphore()
    peers = me * 0
    for way in ways:
        inside, device = near[way]
        peers = peers + jnp.where(inside, 1, 0)

        @pl.when(inside)
        def _():
            pl.semaphore_signal(barrier, inc=1, device_id=(device,), device_id_type=pl.DeviceIdType.MESH)

    def slot(buffers, way):
        kind, start, rows = PLACES[way]
        if kind == "face":
            return buffers[0].at[pl.ds(start, rows)]
        return buffers[1 if kind == "edge" else 2].at[start]

    inboxes = (face_in, edge_in, thin_in)
    for way in WAYS:
        target = slot(inboxes, way)
        if way in near:

            @pl.when(jnp.logical_not(near[way][0]))
            def _():
                target[...] = jnp.zeros(target.shape, target.dtype)
        else:
            target[...] = jnp.zeros(target.shape, target.dtype)
    rim[...] = jnp.zeros_like(rim)

    load_multipoles.wait()
    load_compress.wait()
    compressed = lax.dot_general(
        multipoles[...], compress[...], (((0,), (0,)), ((), ())), preferred_element_type=jnp.float32
    )
    compressed = compressed.astype(jnp.bfloat16).astype(jnp.float32)
    for morton in range(PARENTS):
        place = parent_place(morton)
        field[place * 8 : place * 8 + 8, :] = compressed[morton * 8 : morton * 8 + 8, :]

    def child_of(cx, cy, cz):
        return cx + 2 * cy + 4 * cz

    def line(place, child, count, step):
        return field[pl.ds(place * 8 + child, count, stride=step * 8), :]

    def pack(parts):
        return jnp.concatenate(parts, axis=0).astype(jnp.bfloat16)

    children = [(cx, cy, cz) for cx in (0, 1) for cy in (0, 1) for cz in (0, 1)]

    def pack_own(z):
        for number, bits in enumerate(children):
            rows = line(z * PLANE, child_of(*bits), PLANE, 1)
            own[z * PLANE : (z + 1) * PLANE, number * 128 : number * 128 + 128] = rows.astype(jnp.bfloat16)

    def pack_way(way):
        kind, start, rows = PLACES[way]
        x = SIDE_X - 1 if way[0] > 0 else 0
        y = SIDE_Y - 1 if way[1] > 0 else 0
        z = SIDE_Z - 1 if way[2] > 0 else 0
        place = z * PLANE + y * SIDE_X + x
        if kind == "face":
            for number, bits in enumerate(children):
                child = child_of(*bits)
                if way[0]:
                    parts = [line(x, child, 16, SIDE_X)]
                else:
                    parts = [line(z * PLANE + y * SIDE_X, child, SIDE_X, 1) for z in range(SIDE_Z)]
                face_out[start : start + rows, number * 128 : number * 128 + 128] = pack(parts)
        elif kind == "edge":
            for cy in (0, 1):
                for cz in (0, 1):
                    parts = [line(place, child_of(cx, cy, cz), SIDE_X, 1) for cx in (0, 1)]
                    edge_out[start, :, (cy * 2 + cz) * 128 : (cy * 2 + cz + 1) * 128] = pack(parts)
        else:
            for cz in (0, 1):
                parts = []
                for pair in range(4):
                    child = child_of(pair // 2, pair % 2, cz)
                    if way[2] == 0:
                        parts.append(line(place, child, SIDE_Z, PLANE))
                    elif way[1] == 0:
                        parts.append(line(place, child, SIDE_Y, SIDE_X))
                    else:
                        parts.append(field[place * 8 + child : place * 8 + child + 1, :])
                if way[1] and way[2]:
                    parts.append(jnp.zeros((12, 128), jnp.float32))
                thin_out[start, :, cz * 128 : cz * 128 + 128] = pack(parts)

    def copy_to(way):
        back = tuple(-step for step in way)
        if way[:2] == (0, 0):
            source = own.at[pl.ds(PARENTS - PLANE if way[2] > 0 else 0, PLANE)]
        else:
            source = slot((face_out, edge_out, thin_out), way)
        return pltpu.make_async_remote_copy(
            src_ref=source,
            dst_ref=slot(inboxes, back),
            send_sem=send_sem.at[WAYS.index(way)],
            recv_sem=recv_sem.at[WAYS.index(back)],
            device_id=(near[way][1],),
            device_id_type=pl.DeviceIdType.MESH,
        )

    def send(some):
        for way in some:

            @pl.when(near[way][0])
            def _():
                copy_to(way).start()

    flat_ways = [way for way in ways if way[2] == 0]
    face_ways = [way for way in ways if way[:2] == (0, 0)]
    slant_ways = [way for way in ways if way[2] != 0 and way not in face_ways]
    for way in flat_ways:
        pack_way(way)
    pl.semaphore_wait(barrier, peers)
    send(flat_ways)
    pack_own(0)
    pack_own(SIDE_Z - 1)
    send(face_ways)
    for way in slant_ways:
        pack_way(way)
    send(slant_ways)
    for z in range(1, SIDE_Z - 1):
        pack_own(z)

    def arrive(way):
        @pl.when(near[way][0])
        def _():
            copy_to(tuple(-step for step in way)).wait_recv()

    def spread_plane(plane, pair, values):
        used = sum(value.shape[0] for value in values)
        values = jnp.concatenate(values + [jnp.zeros((256 - used, 256), jnp.bfloat16)], axis=0)
        copies = jnp.dot(pick[plane], values, preferred_element_type=jnp.float32)
        copies = copies.astype(jnp.bfloat16)
        for shift in range(9):
            spread[pair, shift, plane] = copies[shift * PLANE : (shift + 1) * PLANE, :]

    def thin_rows(way, pair, count):
        return thin_in[PLACES[way][1]].astype(jnp.float32)[pair * count : (pair + 1) * count, :]

    def weights_of(sx, sy):
        weights, shifts = [], []
        for dz in (-1, 0, 1):
            entries = [[offsets.get((sx, sy, 2 * dz + cz - pz)) for pz in (0, 1)] for cz in (0, 1)]
            if all(entry is None for row in entries for entry in row):
                continue
            blank = jnp.zeros((128, 128), jnp.bfloat16)
            for row in entries:
                row = [blank if entry is None else held[entry] for entry in row]
                weights.append(jnp.concatenate(row, axis=1))
            shifts.append(dz)
        return weights, shifts

    def interact(levels, group):
        sx, sy = group[0]
        classes = [
            (px, py)
            for px in (0, 1)
            for py in (0, 1)
            if abs((px + sx) // 2) <= 1 and abs((py + sy) // 2) <= 1
        ]
        weights, sources = [], {(kind, z): [] for kind in classes for z in levels}
        for sx, sy in group:
            tiles, shifts = weights_of(sx, sy)
            weights += tiles
            for px, py in classes:
                dx, cx = (px + sx) // 2, (px + sx) % 2
                dy, cy = (py + sy) // 2, (py + sy) % 2
                for z in levels:
                    for dz in shifts:
                        plane = spread[cx * 2 + cy, (dy + 1) * 3 + dx + 1, 1 + z + dz]
                        sources[(px, py), z].append(plane)
        rows = [jnp.concatenate(planes, axis=1) for planes in sources.values()]
        product = jnp.dot(
            jnp.concatenate(rows, axis=0),
            jnp.concatenate(weights, axis=0),
            preferred_element_type=jnp.float32,
        )
        for number, ((px, py), z) in enumerate(sources):
            total[px * 2 + py, z] += product[number * PLANE : (number + 1) * PLANE, :]

    middle = range(-2, 3)

    total[...] = jnp.zeros_like(total)
    load_pick.wait()
    for way in ways:
        if way[2] == 0:
            arrive(way)
    for pair in range(4):
        lanes = slice(pair * 256, pair * 256 + 256)
        for corner, (ex, ey) in enumerate(PAIR_WAYS):
            rim[pair, corner * 4 : corner * 4 + 4, :] = thin_rows((ex, ey, 0), pair, 4)
        corners = rim[pair, 0:16, :].astype(jnp.bfloat16)
        for z in range(SIDE_Z):
            spread_plane(
                z + 1, pair, [own[z * PLANE : (z + 1) * PLANE, lanes], face_in[32:96, lanes], face_in[0:32, lanes], corners]
            )
    for way in ways:
        if way[2] != 0:
            arrive(way)
    for pair in range(4):
        lanes = slice(pair * 256, pair * 256 + 256)
        cx, cy = pair // 2, pair % 2
        for ez in (-1, 1):
            side = 4 + pair * 2 + (ez > 0)
            for number, ey in enumerate((-1, 1)):
                rows = edge_in[PLACES[(0, ey, ez)][1], :, cy * 256 : cy * 256 + 256].astype(jnp.float32)
                rim[side, number * 8 : number * 8 + 8, :] = rows[cx * 8 : cx * 8 + 8, :]
            for number, ex in enumerate((-1, 1)):
                rim[side, 16 + number * 4 : 20 + number * 4, :] = thin_rows((ex, 0, ez), pair, 4)
            for number, (ex, ey) in enumerate(PAIR_WAYS):
                rim[side, 24 + number : 25 + number, :] = thin_rows((ex, ey, ez), pair, 1)
            start = PLACES[(0, 0, ez)][1]
            spread_plane(
                0 if ez < 0 else SIDE_Z + 1, pair,
                [face_in[start : start + PLANE, lanes], rim[side].astype(jnp.bfloat16)],
            )
    levels = range(SIDE_Z)
    for sx in middle:
        load_operators(sx).wait()
        interact(levels, [(sx, sy) for sy in middle])
    for sx in (-3, 3):
        load_operators(sx).wait()
    for far in (-3, 3):
        interact(levels, [(far, sy) for sy in middle])
        interact(levels, [(sx, far) for sx in middle])
        for other in (-3, 3):
            interact(levels, [(far, other)])

    for px in (0, 1):
        for py in (0, 1):
            for pz in (0, 1):
                rows = total[px * 2 + py, :, :, pz * 128 : pz * 128 + 128].reshape(PARENTS, 128)
                field[pl.ds(child_of(px, py, pz), PARENTS, stride=8), :] = rows
    for morton in range(0, PARENTS, 2):
        parts = [field[place * 8 : place * 8 + 8, :] for place in map(parent_place, (morton, morton + 1))]
        out[morton * 8 : morton * 8 + 16, :] = pack(parts)
    for way in ways:

        @pl.when(near[way][0])
        def _():
            copy_to(way).wait_send()


def expand_kernel(expand, reduced, out):
    out[...] = lax.dot_general(
        expand[...], reduced[...], (((1,), (1,)), ((), ())), preferred_element_type=jnp.float32
    )


def local(multipoles, compress, operators, expand):
    cells, rank = multipoles.shape[1], compress.shape[1]
    bit_lists = bits_of_dimension(lax.axis_size("cells"), cells.bit_length() - 1)
    vmem, anywhere = pl.BlockSpec(memory_space=pltpu.VMEM), pl.BlockSpec(memory_space=pl.ANY)
    table = jnp.asarray(picks(), jnp.bfloat16)
    half = jnp.bfloat16
    edges = sum(place[0] == "edge" for place in PLACES.values())
    thins = sum(place[0] == "thin" for place in PLACES.values())
    reduced = pl.pallas_call(
        functools.partial(reduce_kernel, bit_lists),
        out_shape=jax.ShapeDtypeStruct((cells, rank), half),
        in_specs=[anywhere] * 4,
        out_specs=vmem,
        scratch_shapes=[
            pltpu.VMEM(multipoles.shape, half),
            pltpu.VMEM(compress.shape, half),
            pltpu.VMEM(table.shape, half),
            pltpu.VMEM(operators.shape, half),
            pltpu.VMEM((cells, rank), jnp.float32),
            pltpu.VMEM((PARENTS, 8 * rank), half),
            pltpu.VMEM((96, 8 * rank), half),
            pltpu.VMEM((edges, 16, 4 * rank), half),
            pltpu.VMEM((thins, 16, 2 * rank), half),
            pltpu.VMEM((160, 8 * rank), half),
            pltpu.VMEM((edges, 16, 4 * rank), half),
            pltpu.VMEM((thins, 16, 2 * rank), half),
            pltpu.VMEM((12, 32, 2 * rank), jnp.float32),
            pltpu.VMEM((4, 9, SIDE_Z + 2, PLANE, 2 * rank), half),
            pltpu.VMEM((4, SIDE_Z, PLANE, 2 * rank), jnp.float32),
            pltpu.SemaphoreType.DMA((10,)),
            pltpu.SemaphoreType.DMA((len(WAYS),)),
            pltpu.SemaphoreType.DMA((len(WAYS),)),
        ],
        compiler_params=pltpu.CompilerParams(
            collective_id=0, has_side_effects=True, vmem_limit_bytes=62 * 2**20
        ),
        name="interactions",
    )(multipoles, compress, table, operators)
    columns = cells // 2
    return pl.pallas_call(
        expand_kernel,
        out_shape=jax.ShapeDtypeStruct((expand.shape[1], cells), jnp.float32),
        grid=(cells // columns,),
        in_specs=[
            pl.BlockSpec((expand.shape[1], rank), lambda step: (0, 0)),
            pl.BlockSpec((columns, rank), lambda step: (step, 0)),
        ],
        out_specs=pl.BlockSpec((expand.shape[1], columns), lambda step: (0, step)),
        compiler_params=pltpu.CompilerParams(vmem_limit_bytes=62 * 2**20),
        name="expansion",
    )(expand.T, reduced)


def solution(mesh):
    placed = (P(None, "cells"), P(), P(), P())
    return jax.shard_map(
        local, mesh=mesh, in_specs=placed, out_specs=P(None, "cells"), check_vma=False
    )
```

```python
import functools

import jax
import jax.numpy as jnp
import numpy as np
from jax import lax
from jax.experimental import pallas as pl
from jax.experimental.pallas import tpu as pltpu
from jax.sharding import PartitionSpec as P

SIDE_X, SIDE_Y, SIDE_Z = SIDE = (8, 4, 4)
PLANE = SIDE_X * SIDE_Y
PARENTS = PLANE * SIDE_Z
WAYS = [
    (ex, ey, ez)
    for ez in (0, -1, 1)
    for ey in (-1, 0, 1)
    for ex in (-1, 0, 1)
    if (ex, ey, ez) != (0, 0, 0)
]
PLACES = {
    (-1, 0, 0): ("face", 0, 16),
    (1, 0, 0): ("face", 16, 16),
    (0, -1, 0): ("face", 32, 32),
    (0, 1, 0): ("face", 64, 32),
    (0, 0, -1): ("face", 96, 32),
    (0, 0, 1): ("face", 128, 32),
}
for way in WAYS:
    if way not in PLACES:
        kind = "edge" if way[0] == 0 else "thin"
        PLACES[way] = (kind, sum(place[0] == kind for place in PLACES.values()), 16)
PAIR_WAYS = [(ex, ey) for ey in (-1, 1) for ex in (-1, 1)]


def offset_table():
    table = {}
    for sx in range(-3, 4):
        for sy in range(-3, 4):
            for sz in range(-3, 4):
                if max(abs(sx), abs(sy), abs(sz)) >= 2:
                    table[(sx, sy, sz)] = len(table)
    return table


def parent_place(morton):
    coords = [0, 0, 0]
    for bit in range(7):
        coords[bit % 3] += (morton >> bit & 1) << (bit // 3)
    return (coords[2] * SIDE_Y + coords[1]) * SIDE_X + coords[0]


def picks():
    table = np.zeros((SIDE_Z + 2, 9 * PLANE, 256), np.float32)
    for plane in range(SIDE_Z + 2):
        z = plane - 1
        outer = z < 0 or z >= SIDE_Z
        row = 0
        for dy in (-1, 0, 1):
            for dx in (-1, 0, 1):
                for y in range(SIDE_Y):
                    for x in range(SIDE_X):
                        sy, sx = y + dy, x + dx
                        ey = -1 if sy < 0 else 1 if sy >= SIDE_Y else 0
                        ex = -1 if sx < 0 else 1 if sx >= SIDE_X else 0
                        wy, wx = sy % SIDE_Y, sx % SIDE_X
                        if ex == 0 and ey == 0:
                            column = wy * SIDE_X + wx
                        elif ex == 0:
                            column = 32 + (ey > 0) * 8 + wx if outer else 32 + (ey > 0) * 32 + z * 8 + wx
                        elif ey == 0:
                            column = 48 + (ex > 0) * 4 + wy if outer else 96 + (ex > 0) * 16 + z * 4 + wy
                        else:
                            corner = PAIR_WAYS.index((ex, ey))
                            column = 56 + corner if outer else 128 + corner * 4 + z
                        table[plane, row, column] = 1
                        row += 1
    return table


def bits_of_dimension(device_count, local_bits):
    count = device_count.bit_length() - 1
    return [[bit for bit in range(count) if (local_bits + bit) % 3 == dim] for dim in range(3)]


def reduce_kernel(
    bit_lists, multipoles_hbm, compress_hbm, pick_hbm, operators, out,
    multipoles, compress, pick, held, field, own, face_out, edge_out, thin_out,
    face_in, edge_in, thin_in, rim, spread, total, load_sem, send_sem, recv_sem,
):
    offsets = offset_table()
    spans = {}
    for (sx, _, _), number in offsets.items():
        low, high = spans.get(sx, (number, number))
        spans[sx] = (min(low, number), max(high, number))

    def load_operators(sx):
        low, high = spans[sx]
        rows = pl.ds(low, high - low + 1)
        return pltpu.make_async_copy(operators.at[rows], held.at[rows], load_sem.at[sx + 6])

    load_multipoles = pltpu.make_async_copy(multipoles_hbm, multipoles, load_sem.at[0])
    load_compress = pltpu.make_async_copy(compress_hbm, compress, load_sem.at[1])
    load_pick = pltpu.make_async_copy(pick_hbm, pick, load_sem.at[2])
    load_multipoles.start()
    load_compress.start()
    load_pick.start()
    for sx in (-2, -1, 0, 1, 2, -3, 3):
        load_operators(sx).start()

    me = lax.axis_index("cells")
    position = []
    for bits in bit_lists:
        value = me * 0
        for rank, bit in enumerate(bits):
            value = value + (me // 2**bit) % 2 * 2**rank
        position.append(value)

    def neighbour(way):
        inside, device = None, me * 0
        for dim, bits in enumerate(bit_lists):
            place = position[dim] + way[dim]
            if way[dim]:
                fits = (place >= 0) & (place < 2 ** len(bits))
                inside = fits if inside is None else inside & fits
            for rank, bit in enumerate(bits):
                device = device + (place + 2 ** len(bits)) // 2**rank % 2 * 2**bit
        return inside, device

    ways = [way for way in WAYS if all(bits or not step for bits, step in zip(bit_lists, way))]
    near = {way: neighbour(way) for way in ways}
    barrier = pltpu.get_barrier_semaphore()
    peers = me * 0
    for way in ways:
        inside, device = near[way]
        peers = peers + jnp.where(inside, 1, 0)

        @pl.when(inside)
        def _():
            pl.semaphore_signal(barrier, inc=1, device_id=(device,), device_id_type=pl.DeviceIdType.MESH)

    def slot(buffers, way):
        kind, start, rows = PLACES[way]
        if kind == "face":
            return buffers[0].at[pl.ds(start, rows)]
        return buffers[1 if kind == "edge" else 2].at[start]

    inboxes = (face_in, edge_in, thin_in)
    for way in WAYS:
        target = slot(inboxes, way)
        if way in near:

            @pl.when(jnp.logical_not(near[way][0]))
            def _():
                target[...] = jnp.zeros(target.shape, target.dtype)
        else:
            target[...] = jnp.zeros(target.shape, target.dtype)
    rim[...] = jnp.zeros_like(rim)

    load_multipoles.wait()
    load_compress.wait()
    compressed = lax.dot_general(
        multipoles[...], compress[...], (((0,), (0,)), ((), ())), preferred_element_type=jnp.float32
    )
    compressed = compressed.astype(jnp.bfloat16).astype(jnp.float32)
    for morton in range(PARENTS):
        place = parent_place(morton)
        field[place * 8 : place * 8 + 8, :] = compressed[morton * 8 : morton * 8 + 8, :]

    def child_of(cx, cy, cz):
        return cx + 2 * cy + 4 * cz

    def line(place, child, count, step):
        return field[pl.ds(place * 8 + child, count, stride=step * 8), :]

    def pack(parts):
        return jnp.concatenate(parts, axis=0).astype(jnp.bfloat16)

    children = [(cx, cy, cz) for cx in (0, 1) for cy in (0, 1) for cz in (0, 1)]

    def pack_own(z):
        for number, bits in enumerate(children):
            rows = line(z * PLANE, child_of(*bits), PLANE, 1)
            own[z * PLANE : (z + 1) * PLANE, number * 128 : number * 128 + 128] = rows.astype(jnp.bfloat16)

    def pack_way(way):
        kind, start, rows = PLACES[way]
        x = SIDE_X - 1 if way[0] > 0 else 0
        y = SIDE_Y - 1 if way[1] > 0 else 0
        z = SIDE_Z - 1 if way[2] > 0 else 0
        place = z * PLANE + y * SIDE_X + x
        if kind == "face":
            for number, bits in enumerate(children):
                child = child_of(*bits)
                if way[0]:
                    parts = [line(x, child, 16, SIDE_X)]
                else:
                    parts = [line(z * PLANE + y * SIDE_X, child, SIDE_X, 1) for z in range(SIDE_Z)]
                face_out[start : start + rows, number * 128 : number * 128 + 128] = pack(parts)
        elif kind == "edge":
            for cy in (0, 1):
                for cz in (0, 1):
                    parts = [line(place, child_of(cx, cy, cz), SIDE_X, 1) for cx in (0, 1)]
                    edge_out[start, :, (cy * 2 + cz) * 128 : (cy * 2 + cz + 1) * 128] = pack(parts)
        else:
            for cz in (0, 1):
                parts = []
                for pair in range(4):
                    child = child_of(pair // 2, pair % 2, cz)
                    if way[2] == 0:
                        parts.append(line(place, child, SIDE_Z, PLANE))
                    elif way[1] == 0:
                        parts.append(line(place, child, SIDE_Y, SIDE_X))
                    else:
                        parts.append(field[place * 8 + child : place * 8 + child + 1, :])
                if way[1] and way[2]:
                    parts.append(jnp.zeros((12, 128), jnp.float32))
                thin_out[start, :, cz * 128 : cz * 128 + 128] = pack(parts)

    def copy_to(way):
        back = tuple(-step for step in way)
        if way[:2] == (0, 0):
            source = own.at[pl.ds(PARENTS - PLANE if way[2] > 0 else 0, PLANE)]
        else:
            source = slot((face_out, edge_out, thin_out), way)
        return pltpu.make_async_remote_copy(
            src_ref=source,
            dst_ref=slot(inboxes, back),
            send_sem=send_sem.at[WAYS.index(way)],
            recv_sem=recv_sem.at[WAYS.index(back)],
            device_id=(near[way][1],),
            device_id_type=pl.DeviceIdType.MESH,
        )

    def send(some):
        for way in some:

            @pl.when(near[way][0])
            def _():
                copy_to(way).start()

    flat_ways = [way for way in ways if way[2] == 0]
    face_ways = [way for way in ways if way[:2] == (0, 0)]
    slant_ways = [way for way in ways if way[2] != 0 and way not in face_ways]
    for way in flat_ways:
        pack_way(way)
    pl.semaphore_wait(barrier, peers)
    send(flat_ways)
    pack_own(0)
    pack_own(SIDE_Z - 1)
    send(face_ways)
    for way in slant_ways:
        pack_way(way)
    send(slant_ways)
    for z in range(1, SIDE_Z - 1):
        pack_own(z)

    def arrive(way):
        @pl.when(near[way][0])
        def _():
            copy_to(tuple(-step for step in way)).wait_recv()

    def spread_plane(plane, pair, values):
        used = sum(value.shape[0] for value in values)
        values = jnp.concatenate(values + [jnp.zeros((256 - used, 256), jnp.bfloat16)], axis=0)
        copies = jnp.dot(pick[plane], values, preferred_element_type=jnp.float32)
        copies = copies.astype(jnp.bfloat16)
        for shift in range(9):
            spread[pair, shift, plane] = copies[shift * PLANE : (shift + 1) * PLANE, :]

    def thin_rows(way, pair, count):
        return thin_in[PLACES[way][1]].astype(jnp.float32)[pair * count : (pair + 1) * count, :]

    def interact(work, group):
        sx, sy = group[0]
        classes = [
            (px, py)
            for px in (0, 1)
            for py in (0, 1)
            if abs((px + sx) // 2) <= 1 and abs((py + sy) // 2) <= 1
        ]
        for dz, levels in work:
            weights, sources = [], {(kind, z): [] for kind in classes for z in levels}
            for sx, sy in group:
                entries = [[offsets.get((sx, sy, 2 * dz + cz - pz)) for pz in (0, 1)] for cz in (0, 1)]
                if all(entry is None for row in entries for entry in row):
                    continue
                blank = jnp.zeros((128, 128), jnp.bfloat16)
                for row in entries:
                    row = [blank if entry is None else held[entry] for entry in row]
                    weights.append(jnp.concatenate(row, axis=1))
                for px, py in classes:
                    dx, cx = (px + sx) // 2, (px + sx) % 2
                    dy, cy = (py + sy) // 2, (py + sy) % 2
                    for z in levels:
                        plane = spread[cx * 2 + cy, (dy + 1) * 3 + dx + 1, 1 + z + dz]
                        sources[(px, py), z].append(plane)
            if not weights:
                continue
            rows = [jnp.concatenate(planes, axis=1) for planes in sources.values()]
            product = jnp.dot(
                jnp.concatenate(rows, axis=0),
                jnp.concatenate(weights, axis=0),
                preferred_element_type=jnp.float32,
            )
            for number, ((px, py), z) in enumerate(sources):
                total[px * 2 + py, z] += product[number * PLANE : (number + 1) * PLANE, :]

    middle = range(-2, 3)

    total[...] = jnp.zeros_like(total)
    load_pick.wait()
    for way in ways:
        if way[2] == 0:
            arrive(way)
    for pair in range(4):
        lanes = slice(pair * 256, pair * 256 + 256)
        for corner, (ex, ey) in enumerate(PAIR_WAYS):
            rim[pair, corner * 4 : corner * 4 + 4, :] = thin_rows((ex, ey, 0), pair, 4)
        corners = rim[pair, 0:16, :].astype(jnp.bfloat16)
        for z in range(SIDE_Z):
            spread_plane(
                z + 1, pair, [own[z * PLANE : (z + 1) * PLANE, lanes], face_in[32:96, lanes], face_in[0:32, lanes], corners]
            )
    groups = [[(sx, sy) for sy in middle] for sx in middle]
    for far in (-3, 3):
        groups.append([(far, sy) for sy in middle])
        groups.append([(sx, far) for sx in middle])
        groups += [[(far, other)] for other in (-3, 3)]
    inner = [(0, (0, 1, 2, 3)), (-1, (1, 2, 3)), (1, (0, 1, 2))]
    outer = [(-1, (0,)), (1, (3,))]
    for number, group in enumerate(groups):
        if number < len(middle):
            load_operators(middle[number]).wait()
        elif number == len(middle):
            load_operators(-3).wait()
            load_operators(3).wait()
        interact(inner, group)

    for way in ways:
        if way[2] != 0:
            arrive(way)
    for pair in range(4):
        lanes = slice(pair * 256, pair * 256 + 256)
        cx, cy = pair // 2, pair % 2
        for ez in (-1, 1):
            side = 4 + pair * 2 + (ez > 0)
            for number, ey in enumerate((-1, 1)):
                rows = edge_in[PLACES[(0, ey, ez)][1], :, cy * 256 : cy * 256 + 256].astype(jnp.float32)
                rim[side, number * 8 : number * 8 + 8, :] = rows[cx * 8 : cx * 8 + 8, :]
            for number, ex in enumerate((-1, 1)):
                rim[side, 16 + number * 4 : 20 + number * 4, :] = thin_rows((ex, 0, ez), pair, 4)
            for number, (ex, ey) in enumerate(PAIR_WAYS):
                rim[side, 24 + number : 25 + number, :] = thin_rows((ex, ey, ez), pair, 1)
            start = PLACES[(0, 0, ez)][1]
            spread_plane(
                0 if ez < 0 else SIDE_Z + 1, pair,
                [face_in[start : start + PLANE, lanes], rim[side].astype(jnp.bfloat16)],
            )
    for group in groups:
        interact(outer, group)

    for px in (0, 1):
        for py in (0, 1):
            for pz in (0, 1):
                rows = total[px * 2 + py, :, :, pz * 128 : pz * 128 + 128].reshape(PARENTS, 128)
                field[pl.ds(child_of(px, py, pz), PARENTS, stride=8), :] = rows
    for morton in range(0, PARENTS, 2):
        parts = [field[place * 8 : place * 8 + 8, :] for place in map(parent_place, (morton, morton + 1))]
        out[morton * 8 : morton * 8 + 16, :] = pack(parts)
    for way in ways:

        @pl.when(near[way][0])
        def _():
            copy_to(way).wait_send()


def expand_kernel(expand, reduced, out):
    out[...] = lax.dot_general(
        expand[...], reduced[...], (((1,), (1,)), ((), ())), preferred_element_type=jnp.float32
    )


def local(multipoles, compress, operators, expand):
    cells, rank = multipoles.shape[1], compress.shape[1]
    bit_lists = bits_of_dimension(lax.axis_size("cells"), cells.bit_length() - 1)
    vmem, anywhere = pl.BlockSpec(memory_space=pltpu.VMEM), pl.BlockSpec(memory_space=pl.ANY)
    table = jnp.asarray(picks(), jnp.bfloat16)
    half = jnp.bfloat16
    edges = sum(place[0] == "edge" for place in PLACES.values())
    thins = sum(place[0] == "thin" for place in PLACES.values())
    reduced = pl.pallas_call(
        functools.partial(reduce_kernel, bit_lists),
        out_shape=jax.ShapeDtypeStruct((cells, rank), half),
        in_specs=[anywhere] * 4,
        out_specs=vmem,
        scratch_shapes=[
            pltpu.VMEM(multipoles.shape, half),
            pltpu.VMEM(compress.shape, half),
            pltpu.VMEM(table.shape, half),
            pltpu.VMEM(operators.shape, half),
            pltpu.VMEM((cells, rank), jnp.float32),
            pltpu.VMEM((PARENTS, 8 * rank), half),
            pltpu.VMEM((96, 8 * rank), half),
            pltpu.VMEM((edges, 16, 4 * rank), half),
            pltpu.VMEM((thins, 16, 2 * rank), half),
            pltpu.VMEM((160, 8 * rank), half),
            pltpu.VMEM((edges, 16, 4 * rank), half),
            pltpu.VMEM((thins, 16, 2 * rank), half),
            pltpu.VMEM((12, 32, 2 * rank), jnp.float32),
            pltpu.VMEM((4, 9, SIDE_Z + 2, PLANE, 2 * rank), half),
            pltpu.VMEM((4, SIDE_Z, PLANE, 2 * rank), jnp.float32),
            pltpu.SemaphoreType.DMA((10,)),
            pltpu.SemaphoreType.DMA((len(WAYS),)),
            pltpu.SemaphoreType.DMA((len(WAYS),)),
        ],
        compiler_params=pltpu.CompilerParams(
            collective_id=0, has_side_effects=True, vmem_limit_bytes=62 * 2**20
        ),
        name="interactions",
    )(multipoles, compress, table, operators)
    columns = cells // 2
    return pl.pallas_call(
        expand_kernel,
        out_shape=jax.ShapeDtypeStruct((expand.shape[1], cells), jnp.float32),
        grid=(cells // columns,),
        in_specs=[
            pl.BlockSpec((expand.shape[1], rank), lambda step: (0, 0)),
            pl.BlockSpec((columns, rank), lambda step: (step, 0)),
        ],
        out_specs=pl.BlockSpec((expand.shape[1], columns), lambda step: (0, step)),
        compiler_params=pltpu.CompilerParams(vmem_limit_bytes=62 * 2**20),
        name="expansion",
    )(expand.T, reduced)


def solution(mesh):
    placed = (P(None, "cells"), P(), P(), P())
    return jax.shard_map(
        local, mesh=mesh, in_specs=placed, out_specs=P(None, "cells"), check_vma=False
    )
```

```python
import functools

import jax
import jax.numpy as jnp
import numpy as np
from jax import lax
from jax.experimental import pallas as pl
from jax.experimental.pallas import tpu as pltpu
from jax.sharding import PartitionSpec as P

SIDE_X, SIDE_Y, SIDE_Z = SIDE = (8, 4, 4)
PLANE = SIDE_X * SIDE_Y
PARENTS = PLANE * SIDE_Z
WAYS = [
    (ex, ey, ez)
    for ez in (0, -1, 1)
    for ey in (-1, 0, 1)
    for ex in (-1, 0, 1)
    if (ex, ey, ez) != (0, 0, 0)
]
PLACES = {
    (-1, 0, 0): ("face", 0, 16),
    (1, 0, 0): ("face", 16, 16),
    (0, -1, 0): ("face", 32, 32),
    (0, 1, 0): ("face", 64, 32),
    (0, 0, -1): ("face", 96, 32),
    (0, 0, 1): ("face", 128, 32),
}
for way in WAYS:
    if way not in PLACES:
        kind = "edge" if way[0] == 0 else "thin"
        PLACES[way] = (kind, sum(place[0] == kind for place in PLACES.values()), 16)
PAIR_WAYS = [(ex, ey) for ey in (-1, 1) for ex in (-1, 1)]


def offset_table():
    table = {}
    for sx in range(-3, 4):
        for sy in range(-3, 4):
            for sz in range(-3, 4):
                if max(abs(sx), abs(sy), abs(sz)) >= 2:
                    table[(sx, sy, sz)] = len(table)
    return table


def parent_place(morton):
    coords = [0, 0, 0]
    for bit in range(7):
        coords[bit % 3] += (morton >> bit & 1) << (bit // 3)
    return (coords[2] * SIDE_Y + coords[1]) * SIDE_X + coords[0]


def picks():
    table = np.zeros((SIDE_Z + 2, 9 * PLANE, 256), np.float32)
    for plane in range(SIDE_Z + 2):
        z = plane - 1
        outer = z < 0 or z >= SIDE_Z
        row = 0
        for dy in (-1, 0, 1):
            for dx in (-1, 0, 1):
                for y in range(SIDE_Y):
                    for x in range(SIDE_X):
                        sy, sx = y + dy, x + dx
                        ey = -1 if sy < 0 else 1 if sy >= SIDE_Y else 0
                        ex = -1 if sx < 0 else 1 if sx >= SIDE_X else 0
                        wy, wx = sy % SIDE_Y, sx % SIDE_X
                        if ex == 0 and ey == 0:
                            column = wy * SIDE_X + wx
                        elif ex == 0:
                            column = 32 + (ey > 0) * 8 + wx if outer else 32 + (ey > 0) * 32 + z * 8 + wx
                        elif ey == 0:
                            column = 48 + (ex > 0) * 4 + wy if outer else 96 + (ex > 0) * 16 + z * 4 + wy
                        else:
                            corner = PAIR_WAYS.index((ex, ey))
                            column = 56 + corner if outer else 128 + corner * 4 + z
                        table[plane, row, column] = 1
                        row += 1
    return table


def bits_of_dimension(device_count, local_bits):
    count = device_count.bit_length() - 1
    return [[bit for bit in range(count) if (local_bits + bit) % 3 == dim] for dim in range(3)]


def reduce_kernel(
    bit_lists, multipoles_hbm, compress_hbm, pick_hbm, operators, out,
    multipoles, compress, pick, held, field, own, face_out, edge_out, thin_out,
    face_in, edge_in, thin_in, rim, spread, total, load_sem, send_sem, recv_sem,
):
    offsets = offset_table()
    spans = {}
    for (sx, _, _), number in offsets.items():
        low, high = spans.get(sx, (number, number))
        spans[sx] = (min(low, number), max(high, number))

    def load_operators(sx):
        low, high = spans[sx]
        rows = pl.ds(low, high - low + 1)
        return pltpu.make_async_copy(operators.at[rows], held.at[rows], load_sem.at[sx + 6])

    load_multipoles = pltpu.make_async_copy(multipoles_hbm, multipoles, load_sem.at[0])
    load_compress = pltpu.make_async_copy(compress_hbm, compress, load_sem.at[1])
    load_pick = pltpu.make_async_copy(pick_hbm, pick, load_sem.at[2])
    load_multipoles.start()
    load_compress.start()
    load_pick.start()
    for sx in (-2, -1, 0, 1, 2, -3, 3):
        load_operators(sx).start()

    me = lax.axis_index("cells")
    position = []
    for bits in bit_lists:
        value = me * 0
        for rank, bit in enumerate(bits):
            value = value + (me // 2**bit) % 2 * 2**rank
        position.append(value)

    def neighbour(way):
        inside, device = None, me * 0
        for dim, bits in enumerate(bit_lists):
            place = position[dim] + way[dim]
            if way[dim]:
                fits = (place >= 0) & (place < 2 ** len(bits))
                inside = fits if inside is None else inside & fits
            for rank, bit in enumerate(bits):
                device = device + (place + 2 ** len(bits)) // 2**rank % 2 * 2**bit
        return inside, device

    ways = [way for way in WAYS if all(bits or not step for bits, step in zip(bit_lists, way))]
    near = {way: neighbour(way) for way in ways}
    barrier = pltpu.get_barrier_semaphore()
    peers = me * 0
    for way in ways:
        inside, device = near[way]
        peers = peers + jnp.where(inside, 1, 0)

        @pl.when(inside)
        def _():
            pl.semaphore_signal(barrier, inc=1, device_id=(device,), device_id_type=pl.DeviceIdType.MESH)

    def slot(buffers, way):
        kind, start, rows = PLACES[way]
        if kind == "face":
            return buffers[0].at[pl.ds(start, rows)]
        return buffers[1 if kind == "edge" else 2].at[start]

    inboxes = (face_in, edge_in, thin_in)
    for way in WAYS:
        target = slot(inboxes, way)
        if way in near:

            @pl.when(jnp.logical_not(near[way][0]))
            def _():
                target[...] = jnp.zeros(target.shape, target.dtype)
        else:
            target[...] = jnp.zeros(target.shape, target.dtype)
    rim[...] = jnp.zeros_like(rim)

    load_multipoles.wait()
    load_compress.wait()
    compressed = lax.dot_general(
        multipoles[...], compress[...], (((0,), (0,)), ((), ())), preferred_element_type=jnp.float32
    )
    compressed = compressed.astype(jnp.bfloat16).astype(jnp.float32)
    for morton in range(PARENTS):
        place = parent_place(morton)
        field[place * 8 : place * 8 + 8, :] = compressed[morton * 8 : morton * 8 + 8, :]

    def child_of(cx, cy, cz):
        return cx + 2 * cy + 4 * cz

    def line(place, child, count, step):
        return field[pl.ds(place * 8 + child, count, stride=step * 8), :]

    def pack(parts):
        return jnp.concatenate(parts, axis=0).astype(jnp.bfloat16)

    children = [(cx, cy, cz) for cx in (0, 1) for cy in (0, 1) for cz in (0, 1)]

    def pack_own(z):
        for number, bits in enumerate(children):
            rows = line(z * PLANE, child_of(*bits), PLANE, 1)
            own[z * PLANE : (z + 1) * PLANE, number * 128 : number * 128 + 128] = rows.astype(jnp.bfloat16)

    def pack_way(way):
        kind, start, rows = PLACES[way]
        x = SIDE_X - 1 if way[0] > 0 else 0
        y = SIDE_Y - 1 if way[1] > 0 else 0
        z = SIDE_Z - 1 if way[2] > 0 else 0
        place = z * PLANE + y * SIDE_X + x
        if kind == "face":
            for number, bits in enumerate(children):
                child = child_of(*bits)
                if way[0]:
                    parts = [line(x, child, 16, SIDE_X)]
                else:
                    parts = [line(z * PLANE + y * SIDE_X, child, SIDE_X, 1) for z in range(SIDE_Z)]
                face_out[start : start + rows, number * 128 : number * 128 + 128] = pack(parts)
        elif kind == "edge":
            for cy in (0, 1):
                for cz in (0, 1):
                    parts = [line(place, child_of(cx, cy, cz), SIDE_X, 1) for cx in (0, 1)]
                    edge_out[start, :, (cy * 2 + cz) * 128 : (cy * 2 + cz + 1) * 128] = pack(parts)
        else:
            for cz in (0, 1):
                parts = []
                for pair in range(4):
                    child = child_of(pair // 2, pair % 2, cz)
                    if way[2] == 0:
                        parts.append(line(place, child, SIDE_Z, PLANE))
                    elif way[1] == 0:
                        parts.append(line(place, child, SIDE_Y, SIDE_X))
                    else:
                        parts.append(field[place * 8 + child : place * 8 + child + 1, :])
                if way[1] and way[2]:
                    parts.append(jnp.zeros((12, 128), jnp.float32))
                thin_out[start, :, cz * 128 : cz * 128 + 128] = pack(parts)

    def copy_to(way):
        back = tuple(-step for step in way)
        if way[:2] == (0, 0):
            source = own.at[pl.ds(PARENTS - PLANE if way[2] > 0 else 0, PLANE)]
        else:
            source = slot((face_out, edge_out, thin_out), way)
        return pltpu.make_async_remote_copy(
            src_ref=source,
            dst_ref=slot(inboxes, back),
            send_sem=send_sem.at[WAYS.index(way)],
            recv_sem=recv_sem.at[WAYS.index(back)],
            device_id=(near[way][1],),
            device_id_type=pl.DeviceIdType.MESH,
        )

    def send(some):
        for way in some:

            @pl.when(near[way][0])
            def _():
                copy_to(way).start()

    flat_ways = [way for way in ways if way[2] == 0]
    face_ways = [way for way in ways if way[:2] == (0, 0)]
    slant_ways = [way for way in ways if way[2] != 0 and way not in face_ways]
    for way in flat_ways:
        pack_way(way)
    pl.semaphore_wait(barrier, peers)
    send(flat_ways)
    pack_own(0)
    pack_own(SIDE_Z - 1)
    send(face_ways)
    for way in slant_ways:
        pack_way(way)
    send(slant_ways)
    for z in range(1, SIDE_Z - 1):
        pack_own(z)

    def arrive(way):
        @pl.when(near[way][0])
        def _():
            copy_to(tuple(-step for step in way)).wait_recv()

    def spread_plane(plane, pair, values):
        used = sum(value.shape[0] for value in values)
        values = jnp.concatenate(values + [jnp.zeros((256 - used, 256), jnp.bfloat16)], axis=0)
        copies = jnp.dot(pick[plane], values, preferred_element_type=jnp.float32)
        copies = copies.astype(jnp.bfloat16)
        for shift in range(9):
            spread[pair, shift, plane] = copies[shift * PLANE : (shift + 1) * PLANE, :]

    def thin_rows(way, pair, count):
        return thin_in[PLACES[way][1]].astype(jnp.float32)[pair * count : (pair + 1) * count, :]

    def weights_of(sx, sy):
        weights, shifts = [], []
        for dz in (-1, 0, 1):
            entries = [[offsets.get((sx, sy, 2 * dz + cz - pz)) for pz in (0, 1)] for cz in (0, 1)]
            if all(entry is None for row in entries for entry in row):
                continue
            blank = jnp.zeros((128, 128), jnp.bfloat16)
            for row in entries:
                row = [blank if entry is None else held[entry] for entry in row]
                weights.append(jnp.concatenate(row, axis=1))
            shifts.append(dz)
        return weights, shifts

    def interact(levels, group):
        sx, sy = group[0]
        classes = [
            (px, py)
            for px in (0, 1)
            for py in (0, 1)
            if abs((px + sx) // 2) <= 1 and abs((py + sy) // 2) <= 1
        ]
        weights, sources = [], {(kind, z): [] for kind in classes for z in levels}
        for sx, sy in group:
            tiles, shifts = weights_of(sx, sy)
            weights += tiles
            for px, py in classes:
                dx, cx = (px + sx) // 2, (px + sx) % 2
                dy, cy = (py + sy) // 2, (py + sy) % 2
                for z in levels:
                    for dz in shifts:
                        plane = spread[cx * 2 + cy, (dy + 1) * 3 + dx + 1, 1 + z + dz]
                        sources[(px, py), z].append(plane)
        rows = [jnp.concatenate(planes, axis=1) for planes in sources.values()]
        product = jnp.dot(
            jnp.concatenate(rows, axis=0),
            jnp.concatenate(weights, axis=0),
            preferred_element_type=jnp.float32,
        )
        for number, ((px, py), z) in enumerate(sources):
            total[px * 2 + py, z] += product[number * PLANE : (number + 1) * PLANE, :]

    middle = range(-2, 3)

    total[...] = jnp.zeros_like(total)
    load_pick.wait()
    for way in ways:
        if way[2] == 0:
            arrive(way)
    for pair in range(4):
        lanes = slice(pair * 256, pair * 256 + 256)
        for corner, (ex, ey) in enumerate(PAIR_WAYS):
            rim[pair, corner * 4 : corner * 4 + 4, :] = thin_rows((ex, ey, 0), pair, 4)
        corners = rim[pair, 0:16, :].astype(jnp.bfloat16)
        for z in range(SIDE_Z):
            spread_plane(
                z + 1, pair, [own[z * PLANE : (z + 1) * PLANE, lanes], face_in[32:96, lanes], face_in[0:32, lanes], corners]
            )
    for sx in middle:
        load_operators(sx).wait()
        interact((1, 2), [(sx, sy) for sy in middle])

    for way in ways:
        if way[2] != 0:
            arrive(way)
    for pair in range(4):
        lanes = slice(pair * 256, pair * 256 + 256)
        cx, cy = pair // 2, pair % 2
        for ez in (-1, 1):
            side = 4 + pair * 2 + (ez > 0)
            for number, ey in enumerate((-1, 1)):
                rows = edge_in[PLACES[(0, ey, ez)][1], :, cy * 256 : cy * 256 + 256].astype(jnp.float32)
                rim[side, number * 8 : number * 8 + 8, :] = rows[cx * 8 : cx * 8 + 8, :]
            for number, ex in enumerate((-1, 1)):
                rim[side, 16 + number * 4 : 20 + number * 4, :] = thin_rows((ex, 0, ez), pair, 4)
            for number, (ex, ey) in enumerate(PAIR_WAYS):
                rim[side, 24 + number : 25 + number, :] = thin_rows((ex, ey, ez), pair, 1)
            start = PLACES[(0, 0, ez)][1]
            spread_plane(
                0 if ez < 0 else SIDE_Z + 1, pair,
                [face_in[start : start + PLANE, lanes], rim[side].astype(jnp.bfloat16)],
            )
    for sx in middle:
        interact((0, 3), [(sx, sy) for sy in middle])
    levels = range(SIDE_Z)
    for sx in (-3, 3):
        load_operators(sx).wait()
    for far in (-3, 3):
        interact(levels, [(far, sy) for sy in middle])
        interact(levels, [(sx, far) for sx in middle])
        for other in (-3, 3):
            interact(levels, [(far, other)])

    for px in (0, 1):
        for py in (0, 1):
            for pz in (0, 1):
                rows = total[px * 2 + py, :, :, pz * 128 : pz * 128 + 128].reshape(PARENTS, 128)
                field[pl.ds(child_of(px, py, pz), PARENTS, stride=8), :] = rows
    for morton in range(0, PARENTS, 2):
        parts = [field[place * 8 : place * 8 + 8, :] for place in map(parent_place, (morton, morton + 1))]
        out[morton * 8 : morton * 8 + 16, :] = pack(parts)
    for way in ways:

        @pl.when(near[way][0])
        def _():
            copy_to(way).wait_send()


def local(multipoles, compress, operators, expand):
    cells, rank = multipoles.shape[1], compress.shape[1]
    bit_lists = bits_of_dimension(lax.axis_size("cells"), cells.bit_length() - 1)
    vmem, anywhere = pl.BlockSpec(memory_space=pltpu.VMEM), pl.BlockSpec(memory_space=pl.ANY)
    table = jnp.asarray(picks(), jnp.bfloat16)
    half = jnp.bfloat16
    edges = sum(place[0] == "edge" for place in PLACES.values())
    thins = sum(place[0] == "thin" for place in PLACES.values())
    reduced = pl.pallas_call(
        functools.partial(reduce_kernel, bit_lists),
        out_shape=jax.ShapeDtypeStruct((cells, rank), half),
        in_specs=[anywhere] * 4,
        out_specs=vmem,
        scratch_shapes=[
            pltpu.VMEM(multipoles.shape, half),
            pltpu.VMEM(compress.shape, half),
            pltpu.VMEM(table.shape, half),
            pltpu.VMEM(operators.shape, half),
            pltpu.VMEM((cells, rank), jnp.float32),
            pltpu.VMEM((PARENTS, 8 * rank), half),
            pltpu.VMEM((96, 8 * rank), half),
            pltpu.VMEM((edges, 16, 4 * rank), half),
            pltpu.VMEM((thins, 16, 2 * rank), half),
            pltpu.VMEM((160, 8 * rank), half),
            pltpu.VMEM((edges, 16, 4 * rank), half),
            pltpu.VMEM((thins, 16, 2 * rank), half),
            pltpu.VMEM((12, 32, 2 * rank), jnp.float32),
            pltpu.VMEM((4, 9, SIDE_Z + 2, PLANE, 2 * rank), half),
            pltpu.VMEM((4, SIDE_Z, PLANE, 2 * rank), jnp.float32),
            pltpu.SemaphoreType.DMA((10,)),
            pltpu.SemaphoreType.DMA((len(WAYS),)),
            pltpu.SemaphoreType.DMA((len(WAYS),)),
        ],
        compiler_params=pltpu.CompilerParams(
            collective_id=0, has_side_effects=True, vmem_limit_bytes=62 * 2**20
        ),
        name="interactions",
    )(multipoles, compress, table, operators)
    return lax.dot_general(
        expand, reduced, (((0,), (1,)), ((), ())), preferred_element_type=jnp.float32
    )


def solution(mesh):
    placed = (P(None, "cells"), P(), P(), P())
    return jax.shard_map(
        local, mesh=mesh, in_specs=placed, out_specs=P(None, "cells"), check_vma=False
    )
```
